32 devices in a mesh: groups: 2 (over y), morton: 4 (over z), chan: 4 (over x, core).
Axes of the slice: x: 2, y: 2, z: 4, core: 2. Of those that a mesh axis runs over, the one named last changes fastest.
Arguments:
- parents: bfloat16 [16, 256, 512], P(('groups', 'morton'), 'chan'), parts along dimension 0, may hold values from -6 to 6
- up_weight: bfloat16 [8, 256, 128], replicated, may hold values from -0.375 to 0.375
- conv_weight: bfloat16 [27, 128, 128], replicated, may hold values from -0.1875 to 0.1875
- conv_bias: float32 [128], replicated, may hold values from -3 to 3
- child_dest: int32 [128], P(('groups', 'morton')), parts along dimension 0, may hold values from -1 to 31, as said below
- face_nbr: int32 [64, 6], P(('groups', 'morton')), parts along dimension 0, may hold values from -1 to 31, as said below
Outputs:
- children_out: bfloat16 [64, 128, 512], P(('groups', 'morton', 'chan')), parts along dimension 0
The draws below stay inside these ranges and needn't reach their ends.
There are 2 independent parts, one for each index of `groups`. The reference program is written for one: setup_inputs(seed, part) draws one part's arguments, and reference() takes and returns one part's arrays. A program takes and returns all parts, laid end to end along the dimension named above; an argument that names none is the same for every part. Nothing has to cross between parts.
Inputs may be any that keep to these rules, and one draw needn't show every extreme that they name: `child_dest`: candidates are numbered parent-major, octant minor. Kept candidates have positions rising with their number, every position from 0 to 31 is taken once, and the kept children of the parents of one Morton range lie no more than 2 positions outside that range's own 8 positions; in every draw some range passes exactly 2 to the next range and some range exactly 2 to the previous one. `face_nbr`: column k names the kept block across face k (low x, high x, low y, high y, low z, high z) in the window's block grid, or -1 where there is none. Where a range's rows already hold 4 entries naming one other range, its later such entries are also -1 and are treated as empty. The entries of the rows of one Morton range (its 8 positions) that name blocks of one other range number at most 4.
All inputs are finite; a program needn't handle non-finite values.
Results may differ from the reference program's by a relative error of at most 0.0049.
Values may be sent and summed in bfloat16 or wider, within the bound.
A program may use at most 64 MiB of HBM per device.

```python
import jax
import jax.numpy as jnp
from jax import lax

CIN = 256
COUT = 128
VOXELS = 512
FACE_CAP = 4
PB_DEV = 2
MOVE_CAP = 2
CB_DEV = 8
PBLK = 8
CBLK = 32


def alternate(coords, total_bits):
    morton_code = jnp.zeros_like(coords[0])
    for bit_pos in range(total_bits):
        bit_level = bit_pos // 3
        morton_code = morton_code | (coords[bit_pos % 3] >> bit_level & 1) << bit_pos
    return morton_code


def child_layout(key):
    device_total = PBLK // PB_DEV
    cand_dev = 8 * PB_DEV
    parent_bits = max(3, (2 * PBLK - 1).bit_length())
    child_bits = parent_bits + 3
    key_cells, key_shift, key_pick, key_keep = jax.random.split(key, 4)
    parent_cells = jnp.sort(jax.random.permutation(key_cells, 2 ** parent_bits)[:PBLK]).astype(jnp.int32)
    excess = jax.random.randint(key_shift, (device_total,), -MOVE_CAP, MOVE_CAP + 1).astype(jnp.int32)
    picked = jax.random.permutation(key_pick, device_total - 1)[:2]
    excess = excess.at[picked[0]].set(MOVE_CAP).at[picked[1]].set(-MOVE_CAP).at[device_total - 1].set(0)
    previous = jnp.concatenate([jnp.zeros((1,), jnp.int32), excess[:-1]])
    kept_count = CB_DEV + excess - previous
    ranking = jax.vmap(lambda sub_key: jax.random.permutation(sub_key, cand_dev))(jax.random.split(key_keep, device_total))
    is_kept = (ranking < kept_count[:, None]).reshape(-1)
    positions = jnp.where(is_kept, jnp.cumsum(is_kept.astype(jnp.int32)) - 1, -1).astype(jnp.int32)
    child_code = (parent_cells[:, None] * 8 + jnp.arange(8, dtype=jnp.int32)[None, :]).reshape(-1)
    lookup = jnp.full((2 ** child_bits,), -1, jnp.int32).at[child_code].set(positions)
    coords = []
    extents = []
    for axis_pick in range(3):
        coord_value = jnp.zeros_like(child_code)
        for bit_pos in range(axis_pick, child_bits, 3):
            coord_value = coord_value | (child_code >> bit_pos & 1) << bit_pos // 3
        coords.append(coord_value)
        extents.append(2 ** len(range(axis_pick, child_bits, 3)))
    columns = []
    for face_index in range(6):
        axis_pick = face_index // 2
        delta = 1 if face_index % 2 else -1
        moved = coords[axis_pick] + delta
        inside = (moved >= 0) & (moved < extents[axis_pick])
        shifted = list(coords)
        shifted[axis_pick] = jnp.clip(moved, 0, extents[axis_pick] - 1)
        found = lookup[alternate(shifted, child_bits)]
        columns.append(jnp.where(inside, found, -1))
    neighbours = jnp.stack(columns, axis=1).astype(jnp.int32)
    rows_at = jnp.where(is_kept, positions, CBLK)
    face_table = jnp.full((CBLK, 6), -1, jnp.int32).at[rows_at].set(neighbours, mode='drop')
    flat_table = face_table.reshape(device_total, CB_DEV * 6)
    own_range = jnp.arange(device_total, dtype=jnp.int32)[:, None]
    source_range = jnp.where(flat_table >= 0, flat_table // CB_DEV, -1)
    remote = (flat_table >= 0) & (source_range != own_range)
    range_ids = jnp.arange(device_total, dtype=jnp.int32)
    range_hits = (remote[:, :, None] & (source_range[:, :, None] == range_ids[None, None, :])).astype(jnp.int32)
    rank_in = jnp.sum(jnp.cumsum(range_hits, axis=1) * range_hits, axis=2) - 1
    allowed = jnp.logical_not(remote) | (rank_in < FACE_CAP)
    flat_table = jnp.where(allowed, flat_table, -1)
    return (positions, flat_table.reshape(CBLK, 6).astype(jnp.int32))


def draw_child_dest(key, part):
    shared = child_layout(key)
    return shared[0]


def draw_face_nbr(key, part):
    shared = child_layout(key)
    return shared[1]


def shard_levels(stream_key, extent, shards, least, top_value):
    def one(axis_at, blocks):
        draws = jax.random.uniform(jax.random.fold_in(jax.random.fold_in(stream_key, 6), axis_at), (blocks,), jnp.float32, least / len(shards), top_value / len(shards))
        return jnp.repeat(jnp.exp(draws), extent[axis_at] // blocks).reshape((-1,) + (1,) * (len(extent) - axis_at - 1))

    level = one(*shards[0])
    for cut in shards[1:]:
        level = level * one(*cut)
    return level


def gaussian(own_key, dims, scale, limit, cuts=(), kind=jnp.bfloat16):
    values = scale * jax.random.normal(own_key, dims, jnp.float32)
    if cuts:
        values = values * shard_levels(own_key, dims, cuts, -0.22, 0.18)
    return jnp.clip(values, -limit, limit).astype(kind)


def setup_inputs(seed: int = 0, part: int = 0) -> dict:
    keys = jax.random.split(jax.random.key(seed), 7)
    part_keys = jax.random.split(jax.random.fold_in(keys[6], part), 7)
    parents = gaussian(part_keys[0], (PBLK, CIN, VOXELS), 1.0, 6.0, ((0, 4), (1, 4)))
    up_weight = gaussian(keys[1], (8, CIN, COUT), CIN ** -0.5, 0.375)
    conv_weight = gaussian(keys[2], (27, COUT, COUT), (9 * COUT) ** -0.5, 0.1875)
    conv_bias = gaussian(keys[3], (COUT,), 0.5, 3.0, (), jnp.float32)
    child_dest = draw_child_dest(jax.random.fold_in(jax.random.fold_in(keys[6], part), 71), part)
    face_nbr = draw_face_nbr(jax.random.fold_in(jax.random.fold_in(keys[6], part), 71), part)
    return dict(parents=parents, up_weight=up_weight, conv_weight=conv_weight, conv_bias=conv_bias, child_dest=child_dest, face_nbr=face_nbr)


OPPOSITE = (1, 0, 3, 2, 5, 4)


def spread_children(spread):
    block_total = spread.shape[0]
    channels = spread.shape[2]
    grid = spread.reshape(block_total, 2, 2, 2, channels, 8, 8, 8)
    grid = grid.transpose(0, 4, 5, 1, 6, 2, 7, 3).reshape(block_total, channels, 2, 8, 2, 8, 2, 8)
    grid = grid.transpose(0, 6, 4, 2, 1, 3, 5, 7)
    return grid.reshape(block_total * 8, channels, 512)


def face_slabs(blocks):
    block_total = blocks.shape[0]
    channels = blocks.shape[1]
    padded_cube = blocks.reshape(block_total, channels, 8, 8, 8)
    layers = [padded_cube[:, :, 0], padded_cube[:, :, 7], padded_cube[:, :, :, 0], padded_cube[:, :, :, 7], padded_cube[:, :, :, :, 0], padded_cube[:, :, :, :, 7]]
    return jnp.stack([layer.reshape(block_total, channels, 64) for layer in layers], axis=1)


def convolve(blocks, beside, conv_weight, conv_bias):
    block_total = blocks.shape[0]
    channels = blocks.shape[1]
    padded_cube = jnp.pad(blocks.reshape(block_total, channels, 8, 8, 8), ((0, 0), (0, 0), (1, 1), (1, 1), (1, 1)))
    side_faces = beside.reshape(block_total, channels, 6, 8, 8)
    padded_cube = padded_cube.at[:, :, 0, 1:9, 1:9].set(side_faces[:, :, 0])
    padded_cube = padded_cube.at[:, :, 9, 1:9, 1:9].set(side_faces[:, :, 1])
    padded_cube = padded_cube.at[:, :, 1:9, 0, 1:9].set(side_faces[:, :, 2])
    padded_cube = padded_cube.at[:, :, 1:9, 9, 1:9].set(side_faces[:, :, 3])
    padded_cube = padded_cube.at[:, :, 1:9, 1:9, 0].set(side_faces[:, :, 4])
    padded_cube = padded_cube.at[:, :, 1:9, 1:9, 9].set(side_faces[:, :, 5])
    running = jnp.zeros((block_total, conv_weight.shape[2], 512), jnp.float32)
    for shift_x in range(3):
        for shift_y in range(3):
            for shift_z in range(3):
                tap_view = padded_cube[:, :, shift_x:shift_x + 8, shift_y:shift_y + 8, shift_z:shift_z + 8].reshape(block_total, channels, 512)
                weight_tap = conv_weight[9 * shift_x + 3 * shift_y + shift_z]
                running = running + jnp.einsum('cd,bcv->bdv', weight_tap.astype(jnp.float32), tap_view.astype(jnp.float32))
    return jax.nn.silu(running + conv_bias[None, :, None]).astype(jnp.bfloat16)


def reference(parents, up_weight, conv_weight, conv_bias, child_dest, face_nbr):
    range_total = PBLK // PB_DEV

    def lift(parent_part):
        spread = jnp.einsum('ocd,pcv->podv', up_weight.astype(jnp.float32), parent_part.astype(jnp.float32))
        return spread_children(spread).astype(jnp.bfloat16)

    candidates = lax.map(lift, parents.reshape(range_total, PB_DEV, CIN, 512)).reshape(8 * PBLK, COUT, 512)
    target = jnp.where(child_dest >= 0, child_dest, CBLK).astype(jnp.int32)
    kept = jnp.zeros((CBLK, COUT, 512), jnp.bfloat16).at[target].set(candidates, mode="drop")
    layers = face_slabs(kept)
    flipped = jnp.stack([layers[:, slab_index] for slab_index in OPPOSITE], axis=1)
    safe_rows = jnp.clip(face_nbr, 0, CBLK - 1).astype(jnp.int32)
    face_ids = jnp.arange(6, dtype=jnp.int32)[None, :]
    beside = flipped[safe_rows, face_ids]
    beside = jnp.where(face_nbr[:, :, None, None] >= 0, beside, jnp.zeros_like(beside)).astype(jnp.bfloat16)
    beside = beside.transpose(0, 2, 1, 3)
    group_total = CBLK // CB_DEV

    def convolve_group(pair_in):
        return convolve(pair_in[0], pair_in[1], conv_weight, conv_bias)

    result = lax.map(convolve_group, (kept.reshape(group_total, CB_DEV, COUT, 512), beside.reshape(group_total, CB_DEV, COUT, 6, 64)))
    return result.reshape(CBLK, COUT, 512)
```

```python
import functools

import jax
import jax.numpy as jnp
import numpy as np
from jax import lax
from jax.experimental import pallas as pl
from jax.experimental.pallas import tpu as pltpu
from jax.sharding import PartitionSpec as P

MOVE_CAP = 2
FACE_CAP = 4
PIECE = 64
LAYER = 16
MESH = pl.DeviceIdType.MESH


def layer_voxels():
    p, q = np.divmod(np.arange(LAYER), 4)
    return np.stack(
        [48 + 4 * p + q, 4 * p + q, 16 * p + 12 + q, 16 * p + q, 16 * p + 4 * q + 3, 16 * p + 4 * q]
    ).astype(np.int32)


def piece_lanes():
    v = np.arange(PIECE)
    base = 64 * (v // 16) + 8 * (v // 4 % 4) + v % 4
    k = np.arange(8)
    return base.astype(np.int32), (256 * (k % 2) + 32 * (k // 2 % 2) + 4 * (k // 4)).astype(np.int32)


def tables(child_dest, face_nbr, ranges, chans):
    block_count = face_nbr.shape[0]
    own_blocks = block_count // chans
    me = lax.axis_index("morton")
    mine = lax.axis_index("chan")
    base, octant = piece_lanes()
    cand = np.arange(child_dest.shape[0])
    cand_lane = jnp.asarray(512 * (cand // 8) + octant[cand % 8], jnp.int32)

    slots = np.concatenate(
        [
            np.arange(block_count),
            block_count + np.arange(MOVE_CAP),
            np.arange(MOVE_CAP) - MOVE_CAP,
        ]
    ).astype(np.int32)
    wanted = me * block_count + jnp.asarray(slots)
    match = (child_dest[None, :] == wanted[:, None]) & (child_dest >= 0)[None, :]
    found = jnp.sum(jnp.where(match, cand_lane[None, :] + 1, 0), axis=1) - 1
    pick = jnp.where(found[:, None] >= 0, found[:, None] + jnp.asarray(base)[None, :], -1)
    pick = pick.reshape(1, -1)

    entries = face_nbr.reshape(chans, own_blocks * 6)
    count = own_blocks * 6
    face = np.arange(count) % 6
    layer = layer_voxels()
    home = jnp.where(entries >= 0, entries // block_count, -1)
    earlier = np.tril(np.ones((count, count), bool), -1)
    rank = jnp.sum(
        ((home[:, :, None] == home[:, None, :]) & jnp.asarray(earlier)[None]).astype(jnp.int32), axis=2
    )
    offset = jnp.where(home >= 0, lax.rem(home - me + ranges, ranges), -1)
    start = lax.rem(entries, block_count) * PIECE
    far = jnp.arange(1, ranges, dtype=jnp.int32)
    slot_ids = jnp.arange(FACE_CAP, dtype=jnp.int32)
    asks = (offset[None, :, None, :] == far[:, None, None, None]) & (
        rank[None, :, None, :] == slot_ids[None, None, :, None]
    )
    value = start[:, None, :] + jnp.asarray(layer[face].T)[None] + 1
    request = (
        jnp.sum(jnp.where(asks[:, :, :, None, :], value[None, :, None, :, :], 0), axis=-1) - 1
    ).reshape(ranges - 1, 1, chans * FACE_CAP * LAYER)

    def own(a):
        return lax.dynamic_slice_in_dim(a, mine, 1, 0).reshape(own_blocks, 6)

    o_off, o_start, o_rank = own(offset), own(start), own(rank)
    w = np.arange(8)
    inner = (PIECE * (mine * own_blocks + jnp.arange(own_blocks, dtype=jnp.int32)))[:, None] + jnp.asarray(
        (np.arange(16)[:, None] * 4 + w[None, :] // 2).reshape(1, 128).astype(np.int32)
    )
    near = o_off == 0
    spot = jnp.where(
        near, o_start, block_count * PIECE + (o_off - 1) * FACE_CAP * LAYER + o_rank * LAYER
    )
    side16 = (np.arange(4)[:, None] * 4 + w[None, :] // 2).reshape(32).astype(np.int32)
    side_vox = layer[:4][:, side16]
    sides = spot[:, :4, None] + jnp.where(near[:, :4, None], jnp.asarray(side_vox)[None], jnp.asarray(side16))
    sides = jnp.where(o_off[:, :4, None] >= 0, sides, -1).reshape(own_blocks, 128)
    ends = spot[:, 4:, None] + jnp.where(
        near[:, 4:, None], jnp.asarray(layer[4:])[None], jnp.arange(LAYER, dtype=jnp.int32)
    )
    ends = jnp.where(o_off[:, 4:, None] >= 0, ends, -1)
    caps = jnp.where(
        jnp.asarray(w == 0),
        ends[:, 0, :, None],
        jnp.where(jnp.asarray(w == 7), ends[:, 1, :, None], -1),
    ).reshape(own_blocks, 128)
    rows = jnp.concatenate([inner, sides, caps], axis=1).reshape(1, own_blocks * 384)
    return pick, request, rows


def one_hot(depth, target, first=0):
    shape = (depth, target.shape[1])
    lanes = lax.broadcasted_iota(jnp.int32, shape, 0) + first
    return jnp.where(lanes == target, 1.0, 0.0).astype(jnp.bfloat16)


def each(count, body):
    if count <= 4:
        for i in range(count):
            body(i)
    else:
        lax.fori_loop(0, count, lambda i, c: (body(i), c)[1], 0)


def kernel(
    ranges,
    chans,
    parents_ref,
    pick_ref,
    request_ref,
    rows_ref,
    bias_ref,
    up_hbm,
    conv_hbm,
    out_ref,
    up_ref,
    conv_ref,
    moves,
    moved,
    asked,
    held,
    faces_out,
    faces_in,
    far_ref,
    cube,
    cols,
    load_sem,
    ask_send,
    ask_recv,
    move_send,
    move_recv,
    held_send,
    held_recv,
    face_send,
    face_recv,
):
    me = lax.axis_index("morton")
    mine = lax.axis_index("chan")
    total = ranges * chans
    own_blocks = out_ref.shape[0]
    parent_count, depth = parents_ref.shape[0], parents_ref.shape[1]
    half = depth // 2
    width = held.shape[2]

    up_load = pltpu.make_async_copy(up_hbm, up_ref, load_sem.at[0])
    conv_load = pltpu.make_async_copy(conv_hbm, conv_ref, load_sem.at[1])
    up_load.start()
    conv_load.start()

    def at(range_id, chan_id):
        return {"morton": range_id, "chan": chan_id}

    barrier = pltpu.get_barrier_semaphore()
    here = me * chans + mine

    def greet(i):
        other = lax.rem(here + i + 1, total)
        pl.semaphore_signal(
            barrier, inc=1, device_id=at(other // chans, lax.rem(other, chans)), device_id_type=MESH
        )

    each(total - 1, greet)

    gathered = jnp.zeros((depth, pick_ref.shape[1]), jnp.float32)
    for p in range(parent_count):
        gathered = gathered + jnp.dot(
            parents_ref[p],
            one_hot(512, pick_ref[...], 512 * p),
            preferred_element_type=jnp.float32,
        )
    move_width = MOVE_CAP * PIECE
    moves[0] = gathered[:, width : width + move_width].astype(jnp.bfloat16)
    moves[1] = gathered[:, width + move_width :].astype(jnp.bfloat16)
    faces_in[ranges - 1] = jnp.zeros(faces_in.shape[1:], jnp.bfloat16)

    pl.semaphore_wait(barrier, total - 1)

    def move_copy(side):
        other = lax.rem(me + (1 if side == 0 else ranges - 1), ranges)
        return pltpu.make_async_remote_copy(
            src_ref=moves.at[side],
            dst_ref=moved.at[side],
            send_sem=move_send.at[side],
            recv_sem=move_recv.at[side],
            device_id=at(other, mine),
            device_id_type=MESH,
        )

    def ask_copy(m):
        return pltpu.make_async_remote_copy(
            src_ref=request_ref.at[m],
            dst_ref=asked.at[ranges - 2 - m],
            send_sem=ask_send.at[m],
            recv_sem=ask_recv.at[ranges - 2 - m],
            device_id=at(lax.rem(me + m + 1, ranges), mine),
            device_id_type=MESH,
        )

    move_copy(0).start()
    move_copy(1).start()
    each(ranges - 1, lambda m: ask_copy(m).start())

    for side in range(2):
        move_copy(side).wait()
    up_part = jnp.concatenate(
        [moved[0].astype(jnp.float32), jnp.zeros((depth, width - move_width), jnp.float32)], axis=1
    )
    down_part = jnp.concatenate(
        [jnp.zeros((depth, width - move_width), jnp.float32), moved[1].astype(jnp.float32)], axis=1
    )
    blocks = (gathered[:, :width] + up_part + down_part).astype(jnp.bfloat16)
    held[mine] = blocks

    def held_copy(i):
        peer = lax.rem(mine + i + 1, chans)
        return pltpu.make_async_remote_copy(
            src_ref=held.at[mine],
            dst_ref=held.at[mine],
            send_sem=held_send.at[i],
            recv_sem=held_recv.at[i],
            device_id=at(me, peer),
            device_id_type=MESH,
        )

    each(chans - 1, lambda i: held_copy(i).start())

    def face_copy(m, j):
        return pltpu.make_async_remote_copy(
            src_ref=faces_out.at[m, j],
            dst_ref=faces_in.at[ranges - 2 - m, mine],
            send_sem=face_send.at[m, j],
            recv_sem=face_recv.at[ranges - 2 - m, mine],
            device_id=at(lax.rem(me + m + 1, ranges), j),
            device_id_type=MESH,
        )

    def answer(m):
        pltpu.make_async_remote_copy(
            src_ref=request_ref.at[m],
            dst_ref=asked.at[m],
            send_sem=ask_send.at[m],
            recv_sem=ask_recv.at[m],
            device_id=at(lax.rem(me + m + 1, ranges), mine),
            device_id_type=MESH,
        ).wait()
        found = jnp.dot(
            held[mine], one_hot(width, asked[m]), preferred_element_type=jnp.float32
        )
        for j in range(chans):
            part = found[:, PIECE * j : PIECE * (j + 1)]
            faces_out[m, j] = jnp.concatenate([part[:half], part[half:]], axis=1).astype(jnp.bfloat16)
            face_copy(m, j).start()

    each(ranges - 1, answer)

    up_load.wait()
    each(chans - 1, lambda i: held_copy(i).wait_send())

    def held_wait(i):
        source = lax.rem(mine + chans - i - 1, chans)
        pltpu.make_async_remote_copy(
            src_ref=held.at[source],
            dst_ref=held.at[source],
            send_sem=held_send.at[i],
            recv_sem=held_recv.at[i],
            device_id=at(me, source),
            device_id_type=MESH,
        ).wait_recv()

    each(chans - 1, held_wait)
    near = jnp.dot(
        held[...].reshape(chans * depth, width),
        one_hot(width, rows_ref[...]),
        preferred_element_type=jnp.float32,
    )

    def face_wait(m):
        for j in range(chans):
            face_copy(m, j).wait_send()
            pltpu.make_async_remote_copy(
                src_ref=faces_out.at[m, j],
                dst_ref=faces_in.at[m, j],
                send_sem=face_send.at[m, j],
                recv_sem=face_recv.at[m, j],
                device_id=at(lax.rem(me + m + 1, ranges), j),
                device_id_type=MESH,
            ).wait_recv()

    each(ranges - 1, face_wait)

    def unpack(m):
        both = faces_in[m].astype(jnp.float32)
        part = jnp.concatenate([both[:, :, :PIECE], both[:, :, PIECE:]], axis=1)
        return part.reshape(chans * depth, PIECE)

    def widen(i):
        lanes = pl.ds(i * 2 * PIECE if isinstance(i, int) else pl.multiple_of(i * 2 * PIECE, 2 * PIECE), 2 * PIECE)
        far_ref[:, lanes] = jnp.concatenate([unpack(2 * i), unpack(2 * i + 1)], axis=1).astype(jnp.bfloat16)

    each(ranges // 2, widen)
    chosen = near + jnp.dot(
        far_ref[...],
        one_hot(far_ref.shape[1], rows_ref[...], width),
        preferred_element_type=jnp.float32,
    )
    chosen = chosen.T.astype(jnp.bfloat16)

    count = own_blocks * 384
    row = lax.broadcasted_iota(jnp.int32, (count, 128), 0)
    odd = lax.rem(row, 2) == 1
    cap = lax.rem(row // 128, 3) == 2
    high = jnp.logical_xor(odd, cap)
    z_at = lax.rem(lax.broadcasted_iota(jnp.int32, (128, 128), 0), 8)
    lifted = {}
    for ox in range(2):
        for oy in range(2):
            low_z = jnp.dot(chosen, up_ref[4 * ox + 2 * oy], preferred_element_type=jnp.float32)
            high_z = jnp.dot(chosen, up_ref[4 * ox + 2 * oy + 1], preferred_element_type=jnp.float32)
            lifted[ox, oy] = jnp.where(high, high_z, low_z)

    nothing = jnp.zeros((8, 128), jnp.float32)

    def shifts(middle, end):
        below = jnp.where(z_at == 0, end, pltpu.roll(middle, 1, 0))
        above = jnp.where(z_at == 7, end, pltpu.roll(middle, 127, 0))
        return below, middle, above

    conv_load.wait()
    for b in range(own_blocks):
        first = 384 * b
        for ox in range(2):
            for oy in range(2):
                plane = lifted[ox, oy]
                inner = shifts(plane[first : first + 128], plane[first + 256 : first + 384])
                sides = shifts(plane[first + 128 : first + 256], 0.0)
                for dz in range(3):
                    for p in range(4):
                        for q in range(4):
                            at_row = 8 * (4 * p + q)
                            cube[dz, 1 + 2 * p + ox, 1 + 2 * q + oy] = inner[dz][at_row : at_row + 8]
                    for t in range(4):
                        face_x, face_y = 1 - ox, 3 - oy
                        low = 32 * face_x + 8 * t
                        cube[dz, 9 * face_x, 1 + 2 * t + oy] = sides[dz][low : low + 8]
                        low = 32 * face_y + 8 * t
                        cube[dz, 1 + 2 * t + ox, 9 * (face_y - 2)] = sides[dz][low : low + 8]
        for dz in range(3):
            for x in (0, 9):
                for y in (0, 9):
                    cube[dz, x, y] = nothing
        for x in range(10):
            for dy in range(3):
                for dz in range(3):
                    lane = 128 * (3 * dy + dz)
                    cols[x, :, lane : lane + 128] = (
                        cube[dz, x, dy : dy + 8].reshape(64, 128).astype(jnp.bfloat16)
                    )
        total_sum = jnp.zeros((512, 128), jnp.float32) + bias_ref[...]
        for dx in range(3):
            total_sum = total_sum + jnp.dot(
                cols[dx : dx + 8].reshape(512, 1152),
                conv_ref[9 * dx : 9 * dx + 9].reshape(1152, 128),
                preferred_element_type=jnp.float32,
            )
        result = total_sum / (1.0 + jnp.exp(-total_sum))
        out_ref[b] = result.T.astype(jnp.bfloat16)


def per_device(parents, up_weight, conv_weight, conv_bias, child_dest, face_nbr):
    ranges, chans = lax.axis_size("morton"), lax.axis_size("chan")
    block_count = face_nbr.shape[0]
    own_blocks = block_count // chans
    depth = parents.shape[1]
    width = block_count * PIECE
    pick, request, rows = tables(child_dest, face_nbr, ranges, chans)
    vmem = pl.BlockSpec(memory_space=pltpu.VMEM)
    anywhere = pl.BlockSpec(memory_space=pl.ANY)
    bf16 = jnp.bfloat16
    dma = pltpu.SemaphoreType.DMA
    return pl.pallas_call(
        functools.partial(kernel, ranges, chans),
        out_shape=jax.ShapeDtypeStruct((own_blocks, 128, 512), bf16),
        in_specs=[vmem] * 5 + [anywhere] * 2,
        out_specs=vmem,
        scratch_shapes=[
            pltpu.VMEM(up_weight.shape, bf16),
            pltpu.VMEM(conv_weight.shape, bf16),
            pltpu.VMEM((2, depth, MOVE_CAP * PIECE), bf16),
            pltpu.VMEM((2, depth, MOVE_CAP * PIECE), bf16),
            pltpu.VMEM(request.shape, jnp.int32),
            pltpu.VMEM((chans, depth, width), bf16),
            pltpu.VMEM((ranges - 1, chans, depth // 2, 2 * PIECE), bf16),
            pltpu.VMEM((ranges, chans, depth // 2, 2 * PIECE), bf16),
            pltpu.VMEM((chans * depth, ranges * PIECE), bf16),
            pltpu.VMEM((3, 10, 10, 8, 128), jnp.float32),
            pltpu.VMEM((10, 64, 1152), bf16),
            dma((2,)),
            dma((ranges - 1,)),
            dma((ranges - 1,)),
            dma((2,)),
            dma((2,)),
            dma((chans - 1,)),
            dma((chans - 1,)),
            dma((ranges - 1, chans)),
            dma((ranges - 1, chans)),
        ],
        compiler_params=pltpu.CompilerParams(
            collective_id=0, has_side_effects=True, vmem_limit_bytes=40 * 1024 * 1024
        ),
        name="sparse_level",
    )(parents, pick, request, rows, conv_bias.reshape(1, -1), up_weight, conv_weight)


def solution(mesh):
    placed = (
        P(("groups", "morton"), "chan", None),
        P(),
        P(),
        P(),
        P(("groups", "morton")),
        P(("groups", "morton"), None),
    )
    return jax.shard_map(
        per_device,
        mesh=mesh,
        in_specs=placed,
        out_specs=P(("groups", "morton", "chan"), None, None),
        check_vma=False,
    )
```

```python
import functools

import jax
import jax.numpy as jnp
from jax import lax
from jax.experimental import pallas as pl
from jax.experimental.pallas import tpu as pltpu
from jax.sharding import PartitionSpec as P

MOVE_CAP = 2
FACE_CAP = 4
PIECE = 64
LAYER = 16
MESH = pl.DeviceIdType.MESH


def lane_ids(width, rows=1):
    return lax.broadcasted_iota(jnp.int32, (rows, width), 1)


def layer_voxel(face, place):
    p, q = place >> 2, place & 3
    return (
        lambda: 48 + place,
        lambda: place,
        lambda: 16 * p + 12 + q,
        lambda: 16 * p + q,
        lambda: 4 * place + 3,
        lambda: 4 * place,
    )[face]()


def pick_table(dest_ref, ranges, block_count, me):
    slots = block_count + 2 * MOVE_CAP
    lane = lane_ids(slots * PIECE)
    slot, v = lane // PIECE, lane % PIECE
    slot = jnp.where(slot < block_count + MOVE_CAP, slot, slot - slots)
    wanted = me * block_count + slot
    wanted = jnp.where(wanted < 0, -9, wanted)
    base = 64 * (v // 16) + 8 * (v // 4 % 4) + v % 4
    pick = jnp.full(lane.shape, -1, jnp.int32)
    for c in range(dest_ref.shape[0]):
        k = c % 8
        first = 512 * (c // 8) + 256 * (k % 2) + 32 * (k // 2 % 2) + 4 * (k // 4)
        pick = jnp.where(wanted == dest_ref[c], base + first, pick)
    return pick


def request_table(nbr_ref, ranges, chans, me):
    block_count = nbr_ref.shape[0]
    own_blocks = block_count // chans
    shape = (ranges - 1, chans * FACE_CAP * LAYER)
    lane = lane_ids(shape[1], shape[0])
    device, slot, place = lane // (FACE_CAP * LAYER), lane // LAYER % FACE_CAP, lane % LAYER
    home = lax.rem(me + 1 + lax.broadcasted_iota(jnp.int32, shape, 0), ranges)
    layers = [layer_voxel(k, place) for k in range(6)]
    seen = jnp.zeros(shape, jnp.int32)
    ask = jnp.full(shape, -1, jnp.int32)
    for b in range(own_blocks):
        for k in range(6):
            entry = jnp.full(shape, -1, jnp.int32)
            for j in range(chans):
                entry = jnp.where(device == j, nbr_ref[j * own_blocks + b, k], entry)
            start = entry - home * block_count
            hit = (start >= 0) & (start < block_count)
            ask = jnp.where(hit & (seen == slot), start * PIECE + layers[k], ask)
            seen = seen + jnp.where(hit, 1, 0)
    return ask


def row_table(nbr_ref, ranges, chans, me, mine):
    block_count = nbr_ref.shape[0]
    own_blocks = block_count // chans
    width = block_count * PIECE
    lane = lane_ids(128)
    w = lane % 8
    place = 4 * (lane // 8 % 4) + w // 2
    inside, sides, ends = [], [], []
    homes = []
    for b in range(own_blocks):
        inside.append(PIECE * (mine * own_blocks + b) + 4 * (lane // 8) + w // 2)
        side = jnp.full(lane.shape, -1, jnp.int32)
        end = jnp.full(lane.shape, -1, jnp.int32)
        for k in range(6):
            entry = nbr_ref[mine * own_blocks + b, k]
            home = jnp.where(entry >= 0, entry // block_count, -1)
            rank = jnp.int32(0)
            for other in homes:
                rank = rank + jnp.where(other == home, 1, 0)
            homes.append(home)
            near = jnp.where(home == me, 1, 0)
            off = lax.rem(home - me + ranges, ranges)
            far_first = width + (off - 1) * FACE_CAP * LAYER + rank * LAYER
            first = jnp.where(near == 1, (entry - me * block_count) * PIECE, far_first)
            first = jnp.where(home >= 0, first, -(2**20))
            here = place if k < 4 else lane // 8
            target = first + here + near * (layer_voxel(k, here) - here)
            if k < 4:
                side = jnp.where(lane // 32 == k, target, side)
            else:
                end = jnp.where(w == 7 * (k - 4), target, end)
        sides.append(side)
        ends.append(end)
    return inside, sides, ends


def one_hot(depth, target, first=0):
    shape = (depth, target.shape[1])
    lanes = lax.broadcasted_iota(jnp.int32, shape, 0) + first
    return jnp.where(lanes == target, 1.0, 0.0).astype(jnp.bfloat16)


def each(count, body):
    if count <= 4:
        for i in range(count):
            body(i)
    else:
        lax.fori_loop(0, count, lambda i, c: (body(i), c)[1], 0)


def kernel(
    ranges,
    chans,
    dest_ref,
    nbr_ref,
    bias_ref,
    parents_hbm,
    up_hbm,
    conv_hbm,
    out_ref,
    parents_ref,
    up_ref,
    conv_ref,
    moves,
    moved,
    asks,
    asked,
    held,
    faces_out,
    faces_in,
    far_ref,
    cube,
    cols,
    load_sem,
    ask_send,
    ask_recv,
    move_send,
    move_recv,
    held_send,
    held_recv,
    face_send,
    face_recv,
):
    me = lax.axis_index("morton")
    mine = lax.axis_index("chan")
    total = ranges * chans
    own_blocks = out_ref.shape[0]
    block_count = nbr_ref.shape[0]
    parent_count, depth = parents_ref.shape[0], parents_ref.shape[1]
    half = depth // 2
    width = held.shape[2]
    move_width = MOVE_CAP * PIECE

    parents_load = pltpu.make_async_copy(parents_hbm, parents_ref, load_sem.at[2])
    up_load = pltpu.make_async_copy(up_hbm, up_ref, load_sem.at[0])
    conv_load = pltpu.make_async_copy(conv_hbm, conv_ref, load_sem.at[1])
    parents_load.start()
    up_load.start()
    conv_load.start()

    def at(range_id, chan_id):
        return {"morton": range_id, "chan": chan_id}

    barrier = pltpu.get_barrier_semaphore()
    here = me * chans + mine

    def greet(i):
        other = lax.rem(here + i + 1, total)
        pl.semaphore_signal(
            barrier, inc=1, device_id=at(other // chans, lax.rem(other, chans)), device_id_type=MESH
        )

    each(total - 1, greet)

    request = request_table(nbr_ref, ranges, chans, me)
    for m in range(ranges - 1):
        asks[m] = request[m : m + 1]
    pick = pick_table(dest_ref, ranges, block_count, me)
    inside, sides, ends = row_table(nbr_ref, ranges, chans, me, mine)
    inner_rows = jnp.concatenate(inside, axis=1)
    outer_rows = jnp.concatenate(sides + ends, axis=1)

    parents_load.wait()
    gathered = jnp.zeros((depth, pick.shape[1]), jnp.float32)
    for p in range(parent_count):
        gathered = gathered + jnp.dot(
            parents_ref[p], one_hot(512, pick, 512 * p), preferred_element_type=jnp.float32
        )
    gathered = gathered.astype(jnp.bfloat16)
    moves[0] = gathered[:, width : width + move_width]
    moves[1] = gathered[:, width + move_width :]
    held[mine] = gathered[:, :width]
    faces_in[ranges - 1] = jnp.zeros(faces_in.shape[1:], jnp.bfloat16)

    pl.semaphore_wait(barrier, total - 1)

    def ask_copy(m, arrives):
        return pltpu.make_async_remote_copy(
            src_ref=asks.at[m],
            dst_ref=asked.at[arrives],
            send_sem=ask_send.at[m],
            recv_sem=ask_recv.at[arrives],
            device_id=at(lax.rem(me + m + 1, ranges), mine),
            device_id_type=MESH,
        )

    def move_copy(side, i, source):
        other = lax.rem(me + (1 if side == 0 else ranges - 1), ranges)
        return pltpu.make_async_remote_copy(
            src_ref=moves.at[side],
            dst_ref=moved.at[side, source],
            send_sem=move_send.at[side, i],
            recv_sem=move_recv.at[side, i],
            device_id=at(other, lax.rem(mine + i, chans)),
            device_id_type=MESH,
        )

    def held_copy(i, source):
        return pltpu.make_async_remote_copy(
            src_ref=held.at[source],
            dst_ref=held.at[source],
            send_sem=held_send.at[i],
            recv_sem=held_recv.at[i],
            device_id=at(me, lax.rem(mine + i + 1, chans)),
            device_id_type=MESH,
        )

    each(ranges - 1, lambda m: ask_copy(m, ranges - 2 - m).start())
    for i in range(chans):
        for side in range(2):
            move_copy(side, i, mine).start()
    each(chans - 1, lambda i: held_copy(i, mine).start())

    def add_moved(block, low, high):
        first = block[:, :move_width].astype(jnp.float32) + low.astype(jnp.float32)
        last = block[:, width - move_width :].astype(jnp.float32) + high.astype(jnp.float32)
        return jnp.concatenate(
            [
                first.astype(jnp.bfloat16),
                block[:, move_width : width - move_width],
                last.astype(jnp.bfloat16),
            ],
            axis=1,
        )

    for side in range(2):
        move_copy(side, 0, mine).wait_recv()
    own = add_moved(gathered[:, :width], moved[0, mine], moved[1, mine])

    def face_copy(m, j, arrives, source):
        return pltpu.make_async_remote_copy(
            src_ref=faces_out.at[m, j],
            dst_ref=faces_in.at[arrives, source],
            send_sem=face_send.at[m, j],
            recv_sem=face_recv.at[arrives, source],
            device_id=at(lax.rem(me + m + 1, ranges), j),
            device_id_type=MESH,
        )

    def answer(m):
        ask_copy(m, m).wait_recv()
        found = jnp.dot(own, one_hot(width, asked[m]), preferred_element_type=jnp.float32)
        for j in range(chans):
            part = found[:, PIECE * j : PIECE * (j + 1)]
            faces_out[m, j] = jnp.concatenate([part[:half], part[half:]], axis=1).astype(jnp.bfloat16)
            face_copy(m, j, ranges - 2 - m, mine).start()

    each(ranges - 1, answer)

    for i in range(1, chans):
        source = lax.rem(mine + chans - i, chans)
        for side in range(2):
            move_copy(side, i, source).wait_recv()
        held_copy(i - 1, source).wait_recv()
    near = add_moved(
        held[...].reshape(chans * depth, width),
        moved[0].reshape(chans * depth, move_width),
        moved[1].reshape(chans * depth, move_width),
    )

    count = own_blocks * 128
    z_at = lax.rem(lax.broadcasted_iota(jnp.int32, (128, 128), 0), 8)
    odd = lax.rem(lax.broadcasted_iota(jnp.int32, (count, 128), 0), 2) == 1
    outer_high = jnp.concatenate([odd, jnp.logical_not(odd)], axis=0)

    def lift(voxels, high):
        lifted = {}
        for ox in range(2):
            for oy in range(2):
                low_z = jnp.dot(voxels, up_ref[4 * ox + 2 * oy], preferred_element_type=jnp.float32)
                high_z = jnp.dot(voxels, up_ref[4 * ox + 2 * oy + 1], preferred_element_type=jnp.float32)
                lifted[ox, oy] = jnp.where(high, high_z, low_z)
        return lifted

    inner = jnp.dot(near, one_hot(width, inner_rows), preferred_element_type=jnp.float32)
    outer = jnp.dot(near, one_hot(width, outer_rows), preferred_element_type=jnp.float32)
    up_load.wait()
    inner_up = lift(inner.T.astype(jnp.bfloat16), odd)

    def face_wait(m):
        for j in range(chans):
            face_copy(m, j, m, j).wait_recv()

    each(ranges - 1, face_wait)

    def unpack(m):
        both = faces_in[m].astype(jnp.float32)
        part = jnp.concatenate([both[:, :, :PIECE], both[:, :, PIECE:]], axis=1)
        return part.reshape(chans * depth, PIECE)

    def widen(i):
        first = i * 2 * PIECE if isinstance(i, int) else pl.multiple_of(i * 2 * PIECE, 2 * PIECE)
        far_ref[:, pl.ds(first, 2 * PIECE)] = jnp.concatenate(
            [unpack(2 * i), unpack(2 * i + 1)], axis=1
        ).astype(jnp.bfloat16)

    each(ranges // 2, widen)
    outer = outer + jnp.dot(
        far_ref[...],
        one_hot(far_ref.shape[1], outer_rows, width),
        preferred_element_type=jnp.float32,
    )
    outer_up = lift(outer.T.astype(jnp.bfloat16), outer_high)

    nothing = jnp.zeros((8, 128), jnp.float32)

    def shifts(middle, end):
        below = jnp.where(z_at == 0, end, pltpu.roll(middle, 1, 0))
        above = jnp.where(z_at == 7, end, pltpu.roll(middle, 127, 0))
        return below, middle, above

    conv_load.wait()
    for b in range(own_blocks):
        first = 128 * b
        for ox in range(2):
            for oy in range(2):
                outside = outer_up[ox, oy]
                inner = shifts(
                    inner_up[ox, oy][first : first + 128], outside[count + first : count + first + 128]
                )
                sides = shifts(outside[first : first + 128], 0.0)
                for dz in range(3):
                    for p in range(4):
                        for q in range(4):
                            at_row = 8 * (4 * p + q)
                            cube[dz, 1 + 2 * p + ox, 1 + 2 * q + oy] = inner[dz][at_row : at_row + 8]
                    for t in range(4):
                        face_x, face_y = 1 - ox, 3 - oy
                        low = 32 * face_x + 8 * t
                        cube[dz, 9 * face_x, 1 + 2 * t + oy] = sides[dz][low : low + 8]
                        low = 32 * face_y + 8 * t
                        cube[dz, 1 + 2 * t + ox, 9 * (face_y - 2)] = sides[dz][low : low + 8]
        for dz in range(3):
            for x in (0, 9):
                for y in (0, 9):
                    cube[dz, x, y] = nothing
        for x in range(10):
            for dy in range(3):
                for dz in range(3):
                    lane = 128 * (3 * dy + dz)
                    cols[x, :, lane : lane + 128] = (
                        cube[dz, x, dy : dy + 8].reshape(64, 128).astype(jnp.bfloat16)
                    )
        total_sum = jnp.zeros((512, 128), jnp.float32) + bias_ref[...]
        for dx in range(3):
            total_sum = total_sum + jnp.dot(
                cols[dx : dx + 8].reshape(512, 1152),
                conv_ref[9 * dx : 9 * dx + 9].reshape(1152, 128),
                preferred_element_type=jnp.float32,
            )
        result = total_sum / (1.0 + jnp.exp(-total_sum))
        out_ref[b] = result.T.astype(jnp.bfloat16)

    def finish(m):
        ask_copy(m, m).wait_send()
        for j in range(chans):
            face_copy(m, j, m, j).wait_send()

    each(ranges - 1, finish)
    for i in range(chans):
        for side in range(2):
            move_copy(side, i, mine).wait_send()
        if i > 0:
            held_copy(i - 1, mine).wait_send()


def per_device(parents, up_weight, conv_weight, conv_bias, child_dest, face_nbr):
    ranges, chans = lax.axis_size("morton"), lax.axis_size("chan")
    block_count = face_nbr.shape[0]
    own_blocks = block_count // chans
    depth = parents.shape[1]
    width = block_count * PIECE
    vmem = pl.BlockSpec(memory_space=pltpu.VMEM)
    smem = pl.BlockSpec(memory_space=pltpu.SMEM)
    hbm = pl.BlockSpec(memory_space=pltpu.HBM)
    ask_shape = (ranges - 1, 1, chans * FACE_CAP * LAYER)
    bf16 = jnp.bfloat16
    dma = pltpu.SemaphoreType.DMA
    return pl.pallas_call(
        functools.partial(kernel, ranges, chans),
        out_shape=jax.ShapeDtypeStruct((own_blocks, 128, 512), bf16),
        in_specs=[smem] * 2 + [vmem] + [hbm] * 3,
        out_specs=vmem,
        scratch_shapes=[
            pltpu.VMEM(parents.shape, bf16),
            pltpu.VMEM(up_weight.shape, bf16),
            pltpu.VMEM(conv_weight.shape, bf16),
            pltpu.VMEM((2, depth, MOVE_CAP * PIECE), bf16),
            pltpu.VMEM((2, chans, depth, MOVE_CAP * PIECE), bf16),
            pltpu.VMEM(ask_shape, jnp.int32),
            pltpu.VMEM(ask_shape, jnp.int32),
            pltpu.VMEM((chans, depth, width), bf16),
            pltpu.VMEM((ranges - 1, chans, depth // 2, 2 * PIECE), bf16),
            pltpu.VMEM((ranges, chans, depth // 2, 2 * PIECE), bf16),
            pltpu.VMEM((chans * depth, ranges * PIECE), bf16),
            pltpu.VMEM((3, 10, 10, 8, 128), jnp.float32),
            pltpu.VMEM((10, 64, 1152), bf16),
            dma((3,)),
            dma((ranges - 1,)),
            dma((ranges - 1,)),
            dma((2, chans)),
            dma((2, chans)),
            dma((chans - 1,)),
            dma((chans - 1,)),
            dma((ranges - 1, chans)),
            dma((ranges - 1, chans)),
        ],
        compiler_params=pltpu.CompilerParams(
            collective_id=0, has_side_effects=True, vmem_limit_bytes=56 * 1024 * 1024
        ),
        name="sparse_level",
    )(child_dest, face_nbr, conv_bias.reshape(1, -1), parents, up_weight, conv_weight)


def solution(mesh):
    placed = (
        P(("groups", "morton"), "chan", None),
        P(),
        P(),
        P(),
        P(("groups", "morton")),
        P(("groups", "morton"), None),
    )
    return jax.shard_map(
        per_device,
        mesh=mesh,
        in_specs=placed,
        out_specs=P(("groups", "morton", "chan"), None, None),
        check_vma=False,
    )
```

```python
import functools

import jax
import jax.numpy as jnp
from jax import lax
from jax.experimental import pallas as pl
from jax.experimental.pallas import tpu as pltpu
from jax.sharding import PartitionSpec as P

MOVE_CAP = 2
FACE_CAP = 4
PIECE = 64
LAYER = 16
MESH = pl.DeviceIdType.MESH


def lane_ids(width, rows=1):
    return lax.broadcasted_iota(jnp.int32, (rows, width), 1)


def layer_voxel(face, place):
    p, q = place >> 2, place & 3
    return (
        lambda: 48 + place,
        lambda: place,
        lambda: 16 * p + 12 + q,
        lambda: 16 * p + q,
        lambda: 4 * place + 3,
        lambda: 4 * place,
    )[face]()


def pick_table(dest_ref, ranges, block_count, me):
    slots = block_count + 2 * MOVE_CAP
    lane = lane_ids(slots * PIECE)
    slot, v = lane // PIECE, lane % PIECE
    slot = jnp.where(slot < block_count + MOVE_CAP, slot, slot - slots)
    wanted = me * block_count + slot
    wanted = jnp.where(wanted < 0, -9, wanted)
    base = 64 * (v // 16) + 8 * (v // 4 % 4) + v % 4
    pick = jnp.full(lane.shape, -1, jnp.int32)
    for c in range(dest_ref.shape[0]):
        k = c % 8
        first = 512 * (c // 8) + 256 * (k % 2) + 32 * (k // 2 % 2) + 4 * (k // 4)
        pick = jnp.where(wanted == dest_ref[c], base + first, pick)
    return pick


def request_table(nbr_ref, ranges, me):
    block_count = nbr_ref.shape[0]
    shape = (ranges - 1, 2 * FACE_CAP * LAYER)
    lane = lane_ids(shape[1], shape[0])
    slot, place = lane // LAYER, lane % LAYER
    home = lax.rem(me + 1 + lax.broadcasted_iota(jnp.int32, shape, 0), ranges)
    layers = [layer_voxel(k, place) for k in range(6)]
    seen = jnp.zeros(shape, jnp.int32)
    ask = jnp.full(shape, -1, jnp.int32)
    for b in range(block_count):
        for k in range(6):
            start = nbr_ref[b, k] - home * block_count
            hit = (start >= 0) & (start < block_count)
            ask = jnp.where(hit & (seen == slot), start * PIECE + layers[k], ask)
            seen = seen + jnp.where(hit, 1, 0)
    return ask


def inner_table(block_count, own_blocks, mine):
    lane = lane_ids(128)
    return jnp.concatenate(
        [PIECE * (mine * own_blocks + b) + 4 * (lane // 8) + lane % 8 // 2 for b in range(own_blocks)],
        axis=1,
    )


def outer_table(nbr_ref, ranges, own_blocks, me, mine):
    block_count = nbr_ref.shape[0]
    width = block_count * PIECE
    shape = (2 * own_blocks, 128)
    lane = lane_ids(128, shape[0])
    group = lax.broadcasted_iota(jnp.int32, shape, 0)
    w = lane % 8
    end = group >= own_blocks
    block = jnp.where(end, group - own_blocks, group)
    face = jnp.where(end, jnp.where(w == 0, 4, jnp.where(w == 7, 5, 6)), lane // 32)
    place = jnp.where(end, lane // 8, 4 * (lane // 8 % 4) + w // 2)
    order = (mine * own_blocks + block) * 6 + face
    entry = jnp.full(shape, -1, jnp.int32)
    layer = place
    for k in range(6):
        layer = jnp.where(face == k, layer_voxel(k, place), layer)
        for b in range(own_blocks):
            entry = jnp.where(
                (block == b) & (face == k), nbr_ref[mine * own_blocks + b, k], entry
            )
    home = entry >> (block_count.bit_length() - 1)
    rank = jnp.zeros(shape, jnp.int32)
    for b in range(block_count):
        for k in range(6):
            other = nbr_ref[b, k] >> (block_count.bit_length() - 1)
            rank = rank + jnp.where((home == other) & (order > 6 * b + k), 1, 0)
    off = lax.rem(home - me + ranges, ranges)
    target = jnp.where(
        off == 0,
        (entry - me * block_count) * PIECE + layer,
        width + (off - 1) * FACE_CAP * LAYER + rank * LAYER + place,
    )
    target = jnp.where(entry >= 0, target, -1)
    return jnp.concatenate([target[g : g + 1] for g in range(shape[0])], axis=1)


def one_hot(depth, target, first=0):
    shape = (depth, target.shape[1])
    lanes = lax.broadcasted_iota(jnp.int32, shape, 0) + first
    return jnp.where(lanes == target, 1.0, 0.0).astype(jnp.bfloat16)


def each(count, body):
    if count <= 4:
        for i in range(count):
            body(i)
    else:
        lax.fori_loop(0, count, lambda i, c: (body(i), c)[1], 0)


def kernel(
    ranges,
    chans,
    dest_ref,
    nbr_ref,
    bias_ref,
    parents_hbm,
    up_hbm,
    conv_hbm,
    out_ref,
    parents_ref,
    up_ref,
    conv_ref,
    pick_inner,
    pick_outer,
    moves,
    moved,
    asks,
    asked,
    held,
    faces_out,
    faces_in,
    far_ref,
    cube,
    cols,
    load_sem,
    ask_send,
    ask_recv,
    move_send,
    move_recv,
    held_send,
    held_recv,
    face_send,
    face_recv,
    pass_send,
    pass_recv,
):
    me = lax.axis_index("morton")
    mine = lax.axis_index("chan")
    total = ranges * chans
    own_blocks = out_ref.shape[0]
    block_count = nbr_ref.shape[0]
    parent_count, depth = parents_ref.shape[0], parents_ref.shape[1]
    half = depth // 2
    width = held.shape[2]
    move_width = MOVE_CAP * PIECE

    parents_load = pltpu.make_async_copy(parents_hbm, parents_ref, load_sem.at[2])
    up_load = pltpu.make_async_copy(up_hbm, up_ref, load_sem.at[0])
    conv_load = pltpu.make_async_copy(conv_hbm, conv_ref, load_sem.at[1])
    parents_load.start()
    up_load.start()
    conv_load.start()

    def at(range_id, chan_id):
        return {"morton": range_id, "chan": chan_id}

    barrier = pltpu.get_barrier_semaphore()
    here = me * chans + mine

    def greet(i):
        other = lax.rem(here + i + 1, total)
        pl.semaphore_signal(
            barrier, inc=1, device_id=at(other // chans, lax.rem(other, chans)), device_id_type=MESH
        )

    each(total - 1, greet)

    request = request_table(nbr_ref, ranges, me)
    for m in range(ranges - 1):
        asks[m] = request[m : m + 1]

    pl.semaphore_wait(barrier, total - 1)

    def ask_copy(m, arrives):
        return pltpu.make_async_remote_copy(
            src_ref=asks.at[m],
            dst_ref=asked.at[arrives],
            send_sem=ask_send.at[m],
            recv_sem=ask_recv.at[arrives],
            device_id=at(lax.rem(me + m + 1, ranges), mine),
            device_id_type=MESH,
        )

    def move_copy(side, i, source):
        other = lax.rem(me + (1 if side == 0 else ranges - 1), ranges)
        return pltpu.make_async_remote_copy(
            src_ref=moves.at[side],
            dst_ref=moved.at[side, source],
            send_sem=move_send.at[side, i],
            recv_sem=move_recv.at[side, i],
            device_id=at(other, lax.rem(mine + i, chans)),
            device_id_type=MESH,
        )

    def held_copy(i, source):
        return pltpu.make_async_remote_copy(
            src_ref=held.at[source],
            dst_ref=held.at[source],
            send_sem=held_send.at[i],
            recv_sem=held_recv.at[i],
            device_id=at(me, lax.rem(mine + i + 1, chans)),
            device_id_type=MESH,
        )

    each(ranges - 1, lambda m: ask_copy(m, ranges - 2 - m).start())

    pick = pick_table(dest_ref, ranges, block_count, me)
    parents_load.wait()
    gathered = jnp.zeros((depth, pick.shape[1]), jnp.float32)
    for p in range(parent_count):
        gathered = gathered + jnp.dot(
            parents_ref[p], one_hot(512, pick, 512 * p), preferred_element_type=jnp.float32
        )
    gathered = gathered.astype(jnp.bfloat16)
    moves[0] = gathered[:, width : width + move_width]
    moves[1] = gathered[:, width + move_width :]
    held[mine] = gathered[:, :width]

    gives = (me < ranges - 1, me > 0)
    takes = (me > 0, me < ranges - 1)
    for side in range(2):

        @pl.when(gives[side])
        def _():
            for i in range(chans):
                move_copy(side, i, mine).start()

        @pl.when(jnp.logical_not(takes[side]))
        def _():
            moved[side] = jnp.zeros(moved.shape[1:], jnp.bfloat16)

    each(chans - 1, lambda i: held_copy(i, mine).start())

    faces_in[ranges - 1] = jnp.zeros(faces_in.shape[1:], jnp.bfloat16)
    outer_rows = outer_table(nbr_ref, ranges, own_blocks, me, mine)
    pick_outer[...] = one_hot(pick_outer.shape[0], outer_rows)
    pick_inner[...] = one_hot(width, inner_table(block_count, own_blocks, mine))

    def add_moved(block, low, high):
        first = block[:, :move_width].astype(jnp.float32) + low.astype(jnp.float32)
        last = block[:, width - move_width :].astype(jnp.float32) + high.astype(jnp.float32)
        return jnp.concatenate(
            [
                first.astype(jnp.bfloat16),
                block[:, move_width : width - move_width],
                last.astype(jnp.bfloat16),
            ],
            axis=1,
        )

    for side in range(2):

        @pl.when(takes[side])
        def _():
            move_copy(side, 0, mine).wait_recv()

    own = add_moved(gathered[:, :width], moved[0, mine], moved[1, mine])

    def face_copy(m, arrives):
        return pltpu.make_async_remote_copy(
            src_ref=faces_out.at[m],
            dst_ref=faces_in.at[arrives, mine],
            send_sem=face_send.at[m],
            recv_sem=face_recv.at[arrives],
            device_id=at(lax.rem(me + m + 1, ranges), mine),
            device_id_type=MESH,
        )

    def pass_copy(m, i, source):
        return pltpu.make_async_remote_copy(
            src_ref=faces_in.at[m, source],
            dst_ref=faces_in.at[m, source],
            send_sem=pass_send.at[m, i],
            recv_sem=pass_recv.at[m, i],
            device_id=at(me, lax.rem(mine + i + 1, chans)),
            device_id_type=MESH,
        )

    def answer(m):
        ask_copy(m, m).wait_recv()
        found = jnp.dot(own, one_hot(width, asked[m]), preferred_element_type=jnp.float32)
        faces_out[m] = jnp.concatenate([found[:half, :PIECE], found[half:, :PIECE]], axis=1).astype(
            jnp.bfloat16
        )
        face_copy(m, ranges - 2 - m).start()

    each(ranges - 1, answer)

    for i in range(1, chans):
        source = lax.rem(mine + chans - i, chans)
        for side in range(2):

            @pl.when(takes[side])
            def _():
                move_copy(side, i, source).wait_recv()

        held_copy(i - 1, source).wait_recv()
    near = add_moved(
        held[...].reshape(chans * depth, width),
        moved[0].reshape(chans * depth, move_width),
        moved[1].reshape(chans * depth, move_width),
    )

    count = own_blocks * 128
    z_at = lax.rem(lax.broadcasted_iota(jnp.int32, (128, 128), 0), 8)
    odd = lax.rem(lax.broadcasted_iota(jnp.int32, (count, 128), 0), 2) == 1
    outer_high = jnp.concatenate([odd, jnp.logical_not(odd)], axis=0)

    def lift(voxels, high):
        lifted = {}
        for ox in range(2):
            for oy in range(2):
                low_z = jnp.dot(voxels, up_ref[4 * ox + 2 * oy], preferred_element_type=jnp.float32)
                high_z = jnp.dot(voxels, up_ref[4 * ox + 2 * oy + 1], preferred_element_type=jnp.float32)
                lifted[ox, oy] = jnp.where(high, high_z, low_z)
        return lifted

    inner = jnp.dot(near, pick_inner[...], preferred_element_type=jnp.float32)

    def pass_on(m):
        face_copy(m, m).wait_recv()
        for i in range(chans - 1):
            pass_copy(m, i, mine).start()

    each(ranges - 1, pass_on)
    outer = jnp.dot(near, pick_outer[:width], preferred_element_type=jnp.float32)
    up_load.wait()
    inner_up = lift(inner.T.astype(jnp.bfloat16), odd)

    def face_wait(m):
        for i in range(chans - 1):
            pass_copy(m, i, lax.rem(mine + chans - 1 - i, chans)).wait_recv()

    each(ranges - 1, face_wait)

    def unpack(m):
        both = faces_in[m].astype(jnp.float32)
        part = jnp.concatenate([both[:, :, :PIECE], both[:, :, PIECE:]], axis=1)
        return part.reshape(chans * depth, PIECE)

    def widen(i):
        first = i * 2 * PIECE if isinstance(i, int) else pl.multiple_of(i * 2 * PIECE, 2 * PIECE)
        far_ref[:, pl.ds(first, 2 * PIECE)] = jnp.concatenate(
            [unpack(2 * i), unpack(2 * i + 1)], axis=1
        ).astype(jnp.bfloat16)

    each(ranges // 2, widen)
    outer = outer + jnp.dot(
        far_ref[...],
        pick_outer[width:],
        preferred_element_type=jnp.float32,
    )
    outer_up = lift(outer.T.astype(jnp.bfloat16), outer_high)

    nothing = jnp.zeros((8, 128), jnp.float32)

    def shifts(middle, end):
        below = jnp.where(z_at == 0, end, pltpu.roll(middle, 1, 0))
        above = jnp.where(z_at == 7, end, pltpu.roll(middle, 127, 0))
        return below, middle, above

    conv_load.wait()
    for b in range(own_blocks):
        first = 128 * b
        for ox in range(2):
            for oy in range(2):
                outside = outer_up[ox, oy]
                inner = shifts(
                    inner_up[ox, oy][first : first + 128], outside[count + first : count + first + 128]
                )
                sides = shifts(outside[first : first + 128], 0.0)
                for dz in range(3):
                    for p in range(4):
                        for q in range(4):
                            at_row = 8 * (4 * p + q)
                            cube[dz, 1 + 2 * p + ox, 1 + 2 * q + oy] = inner[dz][at_row : at_row + 8]
                    for t in range(4):
                        face_x, face_y = 1 - ox, 3 - oy
                        low = 32 * face_x + 8 * t
                        cube[dz, 9 * face_x, 1 + 2 * t + oy] = sides[dz][low : low + 8]
                        low = 32 * face_y + 8 * t
                        cube[dz, 1 + 2 * t + ox, 9 * (face_y - 2)] = sides[dz][low : low + 8]
        for dz in range(3):
            for x in (0, 9):
                for y in (0, 9):
                    cube[dz, x, y] = nothing
        for x in range(10):
            for dy in range(3):
                for dz in range(3):
                    lane = 128 * (3 * dy + dz)
                    cols[x, :, lane : lane + 128] = (
                        cube[dz, x, dy : dy + 8].reshape(64, 128).astype(jnp.bfloat16)
                    )
        total_sum = jnp.zeros((512, 128), jnp.float32) + bias_ref[...]
        for dx in range(3):
            total_sum = total_sum + jnp.dot(
                cols[dx : dx + 8].reshape(512, 1152),
                conv_ref[9 * dx : 9 * dx + 9].reshape(1152, 128),
                preferred_element_type=jnp.float32,
            )
        out_ref[b] = total_sum.T

    def finish(m):
        ask_copy(m, m).wait_send()
        face_copy(m, m).wait_send()
        for i in range(chans - 1):
            pass_copy(m, i, mine).wait_send()

    each(ranges - 1, finish)
    for i in range(chans):
        for side in range(2):

            @pl.when(gives[side])
            def _():
                move_copy(side, i, mine).wait_send()

        if i > 0:
            held_copy(i - 1, mine).wait_send()


def per_device(parents, up_weight, conv_weight, conv_bias, child_dest, face_nbr):
    ranges, chans = lax.axis_size("morton"), lax.axis_size("chan")
    block_count = face_nbr.shape[0]
    own_blocks = block_count // chans
    depth = parents.shape[1]
    width = block_count * PIECE
    vmem = pl.BlockSpec(memory_space=pltpu.VMEM)
    smem = pl.BlockSpec(memory_space=pltpu.SMEM)
    hbm = pl.BlockSpec(memory_space=pltpu.HBM)
    ask_shape = (ranges - 1, 1, 2 * FACE_CAP * LAYER)
    far_width = ranges * FACE_CAP * LAYER
    bf16 = jnp.bfloat16
    dma = pltpu.SemaphoreType.DMA
    total = pl.pallas_call(
        functools.partial(kernel, ranges, chans),
        out_shape=jax.ShapeDtypeStruct((own_blocks, 128, 512), jnp.float32),
        in_specs=[smem] * 2 + [vmem] + [hbm] * 3,
        out_specs=vmem,
        scratch_shapes=[
            pltpu.VMEM(parents.shape, bf16),
            pltpu.VMEM(up_weight.shape, bf16),
            pltpu.VMEM(conv_weight.shape, bf16),
            pltpu.VMEM((width, own_blocks * 128), bf16),
            pltpu.VMEM((width + far_width, own_blocks * 256), bf16),
            pltpu.VMEM((2, depth, MOVE_CAP * PIECE), bf16),
            pltpu.VMEM((2, chans, depth, MOVE_CAP * PIECE), bf16),
            pltpu.VMEM(ask_shape, jnp.int32),
            pltpu.VMEM(ask_shape, jnp.int32),
            pltpu.VMEM((chans, depth, width), bf16),
            pltpu.VMEM((ranges - 1, depth // 2, 2 * PIECE), bf16),
            pltpu.VMEM((ranges, chans, depth // 2, 2 * PIECE), bf16),
            pltpu.VMEM((chans * depth, ranges * PIECE), bf16),
            pltpu.VMEM((3, 10, 10, 8, 128), jnp.float32),
            pltpu.VMEM((10, 64, 1152), bf16),
            dma((3,)),
            dma((ranges - 1,)),
            dma((ranges - 1,)),
            dma((2, chans)),
            dma((2, chans)),
            dma((chans - 1,)),
            dma((chans - 1,)),
            dma((ranges - 1,)),
            dma((ranges - 1,)),
            dma((ranges - 1, chans - 1)),
            dma((ranges - 1, chans - 1)),
        ],
        compiler_params=pltpu.CompilerParams(
            collective_id=0, has_side_effects=True, vmem_limit_bytes=56 * 1024 * 1024
        ),
        name="sparse_level",
    )(child_dest, face_nbr, conv_bias.reshape(1, -1), parents, up_weight, conv_weight)
    return (total / (1.0 + jnp.exp(-total))).astype(bf16)


def solution(mesh):
    placed = (
        P(("groups", "morton"), "chan", None),
        P(),
        P(),
        P(),
        P(("groups", "morton")),
        P(("groups", "morton"), None),
    )
    return jax.shard_map(
        per_device,
        mesh=mesh,
        in_specs=placed,
        out_specs=P(("groups", "morton", "chan"), None, None),
        check_vma=False,
    )
```

```python
import functools

import jax
import jax.numpy as jnp
from jax import lax
from jax.experimental import pallas as pl
from jax.experimental.pallas import tpu as pltpu
from jax.sharding import PartitionSpec as P

MOVE_CAP = 2
FACE_CAP = 4
PIECE = 64
LAYER = 16
MESH = pl.DeviceIdType.MESH


def lane_ids(width, rows=1):
    return lax.broadcasted_iota(jnp.int32, (rows, width), 1)


def layer_voxel(face, place):
    p, q = place >> 2, place & 3
    return (
        lambda: 48 + place,
        lambda: place,
        lambda: 16 * p + 12 + q,
        lambda: 16 * p + q,
        lambda: 4 * place + 3,
        lambda: 4 * place,
    )[face]()


def pick_table(dest_ref, ranges, block_count, me):
    slots = block_count + 2 * MOVE_CAP
    lane = lane_ids(slots * PIECE)
    slot, v = lane // PIECE, lane % PIECE
    slot = jnp.where(slot < block_count + MOVE_CAP, slot, slot - slots)
    wanted = me * block_count + slot
    wanted = jnp.where(wanted < 0, -9, wanted)
    base = 64 * (v // 16) + 8 * (v // 4 % 4) + v % 4
    pick = jnp.full(lane.shape, -1, jnp.int32)
    for c in range(dest_ref.shape[0]):
        k = c % 8
        first = 512 * (c // 8) + 256 * (k % 2) + 32 * (k // 2 % 2) + 4 * (k // 4)
        pick = jnp.where(wanted == dest_ref[c], base + first, pick)
    return pick


def request_table(nbr_ref, ranges, me):
    block_count = nbr_ref.shape[0]
    shape = (ranges - 1, 2 * FACE_CAP * LAYER)
    lane = lane_ids(shape[1], shape[0])
    slot, place = lane // LAYER, lane % LAYER
    home = lax.rem(me + 1 + lax.broadcasted_iota(jnp.int32, shape, 0), ranges)
    layers = [layer_voxel(k, place) for k in range(6)]
    seen = jnp.zeros(shape, jnp.int32)
    ask = jnp.full(shape, -1, jnp.int32)
    for b in range(block_count):
        for k in range(6):
            start = nbr_ref[b, k] - home * block_count
            hit = (start >= 0) & (start < block_count)
            ask = jnp.where(hit & (seen == slot), start * PIECE + layers[k], ask)
            seen = seen + jnp.where(hit, 1, 0)
    return ask


def inner_table(block_count, own_blocks, mine):
    lane = lane_ids(128)
    return jnp.concatenate(
        [PIECE * (mine * own_blocks + b) + 4 * (lane // 8) + lane % 8 // 2 for b in range(own_blocks)],
        axis=1,
    )


def outer_table(nbr_ref, ranges, own_blocks, me, mine):
    block_count = nbr_ref.shape[0]
    width = block_count * PIECE
    shape = (2 * own_blocks, 128)
    lane = lane_ids(128, shape[0])
    group = lax.broadcasted_iota(jnp.int32, shape, 0)
    w = lane % 8
    end = group >= own_blocks
    block = jnp.where(end, group - own_blocks, group)
    face = jnp.where(end, jnp.where(w == 0, 4, jnp.where(w == 7, 5, 6)), lane // 32)
    place = jnp.where(end, lane // 8, 4 * (lane // 8 % 4) + w // 2)
    order = (mine * own_blocks + block) * 6 + face
    entry = jnp.full(shape, -1, jnp.int32)
    layer = place
    for k in range(6):
        layer = jnp.where(face == k, layer_voxel(k, place), layer)
        for b in range(own_blocks):
            entry = jnp.where(
                (block == b) & (face == k), nbr_ref[mine * own_blocks + b, k], entry
            )
    home = entry >> (block_count.bit_length() - 1)
    rank = jnp.zeros(shape, jnp.int32)
    for b in range(block_count):
        for k in range(6):
            other = nbr_ref[b, k] >> (block_count.bit_length() - 1)
            rank = rank + jnp.where((home == other) & (order > 6 * b + k), 1, 0)
    off = lax.rem(home - me + ranges, ranges)
    target = jnp.where(
        off == 0,
        (entry - me * block_count) * PIECE + layer,
        width + (off - 1) * FACE_CAP * LAYER + rank * LAYER + place,
    )
    target = jnp.where(entry >= 0, target, -1)
    return jnp.concatenate([target[g : g + 1] for g in range(shape[0])], axis=1)


def one_hot(depth, target, first=0):
    shape = (depth, target.shape[1])
    lanes = lax.broadcasted_iota(jnp.int32, shape, 0) + first
    return jnp.where(lanes == target, 1.0, 0.0).astype(jnp.bfloat16)


def each(count, body):
    if count <= 4:
        for i in range(count):
            body(i)
    else:
        lax.fori_loop(0, count, lambda i, c: (body(i), c)[1], 0)


def kernel(
    ranges,
    chans,
    dest_ref,
    nbr_ref,
    bias_ref,
    parents_hbm,
    up_hbm,
    conv_hbm,
    out_ref,
    parents_ref,
    up_ref,
    conv_ref,
    pick_inner,
    pick_outer,
    moves,
    moved,
    asks,
    asked,
    held,
    faces_out,
    faces_in,
    far_ref,
    cube,
    cols,
    load_sem,
    ask_send,
    ask_recv,
    move_send,
    move_recv,
    held_send,
    held_recv,
    face_send,
    face_recv,
):
    me = lax.axis_index("morton")
    mine = lax.axis_index("chan")
    total = ranges * chans
    own_blocks = out_ref.shape[0]
    block_count = nbr_ref.shape[0]
    parent_count, depth = parents_ref.shape[0], parents_ref.shape[1]
    half = depth // 2
    width = held.shape[2]
    move_width = MOVE_CAP * PIECE

    parents_load = pltpu.make_async_copy(parents_hbm, parents_ref, load_sem.at[2])
    up_load = pltpu.make_async_copy(up_hbm, up_ref, load_sem.at[0])
    conv_load = pltpu.make_async_copy(conv_hbm, conv_ref, load_sem.at[1])
    parents_load.start()
    up_load.start()
    conv_load.start()

    def at(range_id, chan_id):
        return {"morton": range_id, "chan": chan_id}

    barrier = pltpu.get_barrier_semaphore()
    here = me * chans + mine

    def greet(i):
        other = lax.rem(here + i + 1, total)
        pl.semaphore_signal(
            barrier, inc=1, device_id=at(other // chans, lax.rem(other, chans)), device_id_type=MESH
        )

    each(total - 1, greet)

    request = request_table(nbr_ref, ranges, me)
    for m in range(ranges - 1):
        asks[m] = request[m : m + 1]
    pick = pick_table(dest_ref, ranges, block_count, me)

    def gather(columns):
        found = jnp.zeros((depth, columns.shape[1]), jnp.float32)
        for p in range(parent_count):
            found = found + jnp.dot(
                parents_ref[p], one_hot(512, columns, 512 * p), preferred_element_type=jnp.float32
            )
        return found.astype(jnp.bfloat16)

    parents_load.wait()
    passed = gather(pick[:, width:])
    moves[0] = passed[:, :move_width]
    moves[1] = passed[:, move_width:]

    pl.semaphore_wait(barrier, total - 1)

    def ask_copy(m, arrives):
        return pltpu.make_async_remote_copy(
            src_ref=asks.at[m],
            dst_ref=asked.at[arrives],
            send_sem=ask_send.at[m],
            recv_sem=ask_recv.at[arrives],
            device_id=at(lax.rem(me + m + 1, ranges), mine),
            device_id_type=MESH,
        )

    def move_copy(side, i, source):
        other = lax.rem(me + (1 if side == 0 else ranges - 1), ranges)
        return pltpu.make_async_remote_copy(
            src_ref=moves.at[side],
            dst_ref=moved.at[side, source],
            send_sem=move_send.at[side, i],
            recv_sem=move_recv.at[side, i],
            device_id=at(other, lax.rem(mine + i, chans)),
            device_id_type=MESH,
        )

    def held_copy(i, source):
        return pltpu.make_async_remote_copy(
            src_ref=held.at[source],
            dst_ref=held.at[source],
            send_sem=held_send.at[i],
            recv_sem=held_recv.at[i],
            device_id=at(me, lax.rem(mine + i + 1, chans)),
            device_id_type=MESH,
        )

    each(ranges - 1, lambda m: ask_copy(m, ranges - 2 - m).start())

    gives = (me < ranges - 1, me > 0)
    takes = (me > 0, me < ranges - 1)
    for side in range(2):

        @pl.when(gives[side])
        def _():
            for i in range(chans):
                move_copy(side, i, mine).start()

        @pl.when(jnp.logical_not(takes[side]))
        def _():
            moved[side] = jnp.zeros(moved.shape[1:], jnp.bfloat16)

    gathered = gather(pick[:, :width])
    held[mine] = gathered
    each(chans - 1, lambda i: held_copy(i, mine).start())

    faces_in[ranges - 1] = jnp.zeros(faces_in.shape[1:], jnp.bfloat16)
    outer_rows = outer_table(nbr_ref, ranges, own_blocks, me, mine)
    pick_outer[...] = one_hot(pick_outer.shape[0], outer_rows)
    pick_inner[...] = one_hot(width, inner_table(block_count, own_blocks, mine))

    def add_moved(block, low, high):
        first = block[:, :move_width].astype(jnp.float32) + low.astype(jnp.float32)
        last = block[:, width - move_width :].astype(jnp.float32) + high.astype(jnp.float32)
        return jnp.concatenate(
            [
                first.astype(jnp.bfloat16),
                block[:, move_width : width - move_width],
                last.astype(jnp.bfloat16),
            ],
            axis=1,
        )

    for side in range(2):

        @pl.when(takes[side])
        def _():
            move_copy(side, 0, mine).wait_recv()

    own = add_moved(gathered, moved[0, mine], moved[1, mine])

    def face_copy(m, i, arrives, source):
        return pltpu.make_async_remote_copy(
            src_ref=faces_out.at[m],
            dst_ref=faces_in.at[arrives, source],
            send_sem=face_send.at[m, i],
            recv_sem=face_recv.at[arrives, i],
            device_id=at(lax.rem(me + m + 1, ranges), lax.rem(mine + i, chans)),
            device_id_type=MESH,
        )

    def answer(first, count):
        ask = []
        for m in range(count):
            ask_copy(first + m, first + m).wait_recv()
            ask.append(asked[first + m][:, :PIECE])
        found = jnp.dot(
            own, one_hot(width, jnp.concatenate(ask, axis=1)), preferred_element_type=jnp.float32
        )
        for m in range(count):
            part = found[:, PIECE * m : PIECE * (m + 1)]
            faces_out[first + m] = jnp.concatenate([part[:half], part[half:]], axis=1).astype(
                jnp.bfloat16
            )
            for i in range(chans):
                face_copy(first + m, i, ranges - 2 - first - m, mine).start()

    if ranges <= 4:
        answer(0, ranges - 1)
    else:
        each(ranges - 1, lambda m: answer(m, 1))

    for i in range(1, chans):
        source = lax.rem(mine + chans - i, chans)
        for side in range(2):

            @pl.when(takes[side])
            def _():
                move_copy(side, i, source).wait_recv()

        held_copy(i - 1, source).wait_recv()
    near = add_moved(
        held[...].reshape(chans * depth, width),
        moved[0].reshape(chans * depth, move_width),
        moved[1].reshape(chans * depth, move_width),
    )

    count = own_blocks * 128
    z_at = lax.rem(lax.broadcasted_iota(jnp.int32, (128, 128), 0), 8)
    odd = lax.rem(lax.broadcasted_iota(jnp.int32, (count, 128), 0), 2) == 1
    outer_high = jnp.concatenate([odd, jnp.logical_not(odd)], axis=0)

    def lift(voxels, high):
        lifted = {}
        for ox in range(2):
            for oy in range(2):
                low_z = jnp.dot(voxels, up_ref[4 * ox + 2 * oy], preferred_element_type=jnp.float32)
                high_z = jnp.dot(voxels, up_ref[4 * ox + 2 * oy + 1], preferred_element_type=jnp.float32)
                lifted[ox, oy] = jnp.where(high, high_z, low_z)
        return lifted

    inner = jnp.dot(near, pick_inner[...], preferred_element_type=jnp.float32)

    outer = jnp.dot(near, pick_outer[:width], preferred_element_type=jnp.float32)
    up_load.wait()
    inner_up = lift(inner.T.astype(jnp.bfloat16), odd)

    def face_wait(m):
        for i in range(chans):
            face_copy(m, i, m, lax.rem(mine + chans - i, chans)).wait_recv()

    each(ranges - 1, face_wait)

    def unpack(m):
        both = faces_in[m].astype(jnp.float32)
        part = jnp.concatenate([both[:, :, :PIECE], both[:, :, PIECE:]], axis=1)
        return part.reshape(chans * depth, PIECE)

    def widen(i):
        first = i * 2 * PIECE if isinstance(i, int) else pl.multiple_of(i * 2 * PIECE, 2 * PIECE)
        far_ref[:, pl.ds(first, 2 * PIECE)] = jnp.concatenate(
            [unpack(2 * i), unpack(2 * i + 1)], axis=1
        ).astype(jnp.bfloat16)

    each(ranges // 2, widen)
    outer = outer + jnp.dot(
        far_ref[...],
        pick_outer[width:],
        preferred_element_type=jnp.float32,
    )
    outer_up = lift(outer.T.astype(jnp.bfloat16), outer_high)

    nothing = jnp.zeros((8, 128), jnp.float32)

    def shifts(middle, end):
        below = jnp.where(z_at == 0, end, pltpu.roll(middle, 1, 0))
        above = jnp.where(z_at == 7, end, pltpu.roll(middle, 127, 0))
        return below, middle, above

    conv_load.wait()
    for b in range(own_blocks):
        first = 128 * b
        for ox in range(2):
            for oy in range(2):
                outside = outer_up[ox, oy]
                inner = shifts(
                    inner_up[ox, oy][first : first + 128], outside[count + first : count + first + 128]
                )
                sides = shifts(outside[first : first + 128], 0.0)
                for dz in range(3):
                    for p in range(4):
                        for q in range(4):
                            at_row = 8 * (4 * p + q)
                            cube[dz, 1 + 2 * p + ox, 1 + 2 * q + oy] = inner[dz][at_row : at_row + 8]
                    for t in range(4):
                        face_x, face_y = 1 - ox, 3 - oy
                        low = 32 * face_x + 8 * t
                        cube[dz, 9 * face_x, 1 + 2 * t + oy] = sides[dz][low : low + 8]
                        low = 32 * face_y + 8 * t
                        cube[dz, 1 + 2 * t + ox, 9 * (face_y - 2)] = sides[dz][low : low + 8]
        for dz in range(3):
            for x in (0, 9):
                for y in (0, 9):
                    cube[dz, x, y] = nothing
        for x in range(10):
            for dy in range(3):
                for dz in range(3):
                    lane = 128 * (3 * dy + dz)
                    cols[x, :, lane : lane + 128] = (
                        cube[dz, x, dy : dy + 8].reshape(64, 128).astype(jnp.bfloat16)
                    )
        total_sum = jnp.zeros((512, 128), jnp.float32) + bias_ref[...]
        for dx in range(3):
            total_sum = total_sum + jnp.dot(
                cols[dx : dx + 8].reshape(512, 1152),
                conv_ref[9 * dx : 9 * dx + 9].reshape(1152, 128),
                preferred_element_type=jnp.float32,
            )
        result = total_sum / (1.0 + jnp.exp(-total_sum))
        out_ref[b] = result.T.astype(jnp.bfloat16)

    def finish(m):
        ask_copy(m, m).wait_send()
        for i in range(chans):
            face_copy(m, i, m, mine).wait_send()

    each(ranges - 1, finish)
    for i in range(chans):
        for side in range(2):

            @pl.when(gives[side])
            def _():
                move_copy(side, i, mine).wait_send()

        if i > 0:
            held_copy(i - 1, mine).wait_send()


def per_device(parents, up_weight, conv_weight, conv_bias, child_dest, face_nbr):
    ranges, chans = lax.axis_size("morton"), lax.axis_size("chan")
    block_count = face_nbr.shape[0]
    own_blocks = block_count // chans
    depth = parents.shape[1]
    width = block_count * PIECE
    vmem = pl.BlockSpec(memory_space=pltpu.VMEM)
    smem = pl.BlockSpec(memory_space=pltpu.SMEM)
    hbm = pl.BlockSpec(memory_space=pltpu.HBM)
    ask_shape = (ranges - 1, 1, 2 * FACE_CAP * LAYER)
    far_width = ranges * FACE_CAP * LAYER
    bf16 = jnp.bfloat16
    dma = pltpu.SemaphoreType.DMA
    return pl.pallas_call(
        functools.partial(kernel, ranges, chans),
        out_shape=pltpu.VMEM((own_blocks, 128, 512), bf16),
        in_specs=[smem] * 2 + [vmem] + [hbm] * 3,
        out_specs=vmem,
        scratch_shapes=[
            pltpu.VMEM(parents.shape, bf16),
            pltpu.VMEM(up_weight.shape, bf16),
            pltpu.VMEM(conv_weight.shape, bf16),
            pltpu.VMEM((width, own_blocks * 128), bf16),
            pltpu.VMEM((width + far_width, own_blocks * 256), bf16),
            pltpu.VMEM((2, depth, MOVE_CAP * PIECE), bf16),
            pltpu.VMEM((2, chans, depth, MOVE_CAP * PIECE), bf16),
            pltpu.VMEM(ask_shape, jnp.int32),
            pltpu.VMEM(ask_shape, jnp.int32),
            pltpu.VMEM((chans, depth, width), bf16),
            pltpu.VMEM((ranges - 1, depth // 2, 2 * PIECE), bf16),
            pltpu.VMEM((ranges, chans, depth // 2, 2 * PIECE), bf16),
            pltpu.VMEM((chans * depth, ranges * PIECE), bf16),
            pltpu.VMEM((3, 10, 10, 8, 128), jnp.float32),
            pltpu.VMEM((10, 64, 1152), bf16),
            dma((3,)),
            dma((ranges - 1,)),
            dma((ranges - 1,)),
            dma((2, chans)),
            dma((2, chans)),
            dma((chans - 1,)),
            dma((chans - 1,)),
            dma((ranges - 1, chans)),
            dma((ranges - 1, chans)),
        ],
        compiler_params=pltpu.CompilerParams(
            collective_id=0, has_side_effects=True, vmem_limit_bytes=56 * 1024 * 1024
        ),
        name="sparse_level",
    )(child_dest, face_nbr, conv_bias.reshape(1, -1), parents, up_weight, conv_weight)


def solution(mesh):
    placed = (
        P(("groups", "morton"), "chan", None),
        P(),
        P(),
        P(),
        P(("groups", "morton")),
        P(("groups", "morton"), None),
    )
    return jax.shard_map(
        per_device,
        mesh=mesh,
        in_specs=placed,
        out_specs=P(("groups", "morton", "chan"), None, None),
        check_vma=False,
    )
```

```python
import functools

import jax
import jax.numpy as jnp
from jax import lax
from jax.experimental import pallas as pl
from jax.experimental.pallas import tpu as pltpu
from jax.sharding import PartitionSpec as P

MOVE_CAP = 2
FACE_CAP = 4
PIECE = 64
LAYER = 16
MESH = pl.DeviceIdType.MESH


def lane_ids(width, rows=1):
    return lax.broadcasted_iota(jnp.int32, (rows, width), 1)


def layer_voxel(face, place):
    p, q = place >> 2, place & 3
    return (
        lambda: 48 + place,
        lambda: place,
        lambda: 16 * p + 12 + q,
        lambda: 16 * p + q,
        lambda: 4 * place + 3,
        lambda: 4 * place,
    )[face]()


def pick_table(dest_ref, ranges, block_count, me):
    slots = block_count + 2 * MOVE_CAP
    lane = lane_ids(slots * PIECE)
    slot, v = lane // PIECE, lane % PIECE
    slot = jnp.where(slot < block_count + MOVE_CAP, slot, slot - slots)
    wanted = me * block_count + slot
    wanted = jnp.where(wanted < 0, -9, wanted)
    base = 64 * (v // 16) + 8 * (v // 4 % 4) + v % 4
    pick = jnp.full(lane.shape, -1, jnp.int32)
    for c in range(dest_ref.shape[0]):
        k = c % 8
        first = 512 * (c // 8) + 256 * (k % 2) + 32 * (k // 2 % 2) + 4 * (k // 4)
        pick = jnp.where(wanted == dest_ref[c], base + first, pick)
    return pick


def request_table(nbr_ref, ranges, me):
    block_count = nbr_ref.shape[0]
    shape = (ranges - 1, 2 * FACE_CAP * LAYER)
    lane = lane_ids(shape[1], shape[0])
    slot, place = lane // LAYER, lane % LAYER
    home = lax.rem(me + 1 + lax.broadcasted_iota(jnp.int32, shape, 0), ranges)
    layers = [layer_voxel(k, place) for k in range(6)]
    seen = jnp.zeros(shape, jnp.int32)
    ask = jnp.full(shape, -1, jnp.int32)
    for b in range(block_count):
        for k in range(6):
            start = nbr_ref[b, k] - home * block_count
            hit = (start >= 0) & (start < block_count)
            ask = jnp.where(hit & (seen == slot), start * PIECE + layers[k], ask)
            seen = seen + jnp.where(hit, 1, 0)
    return ask


def inner_table(block_count, own_blocks, mine):
    lane = lane_ids(128)
    return jnp.concatenate(
        [PIECE * (mine * own_blocks + b) + 4 * (lane // 8) + lane % 8 // 2 for b in range(own_blocks)],
        axis=1,
    )


def outer_table(nbr_ref, ranges, own_blocks, me, mine):
    block_count = nbr_ref.shape[0]
    width = block_count * PIECE
    shape = (2 * own_blocks, 128)
    lane = lane_ids(128, shape[0])
    group = lax.broadcasted_iota(jnp.int32, shape, 0)
    w = lane % 8
    end = group >= own_blocks
    block = jnp.where(end, group - own_blocks, group)
    face = jnp.where(end, jnp.where(w == 0, 4, jnp.where(w == 7, 5, 6)), lane // 32)
    place = jnp.where(end, lane // 8, 4 * (lane // 8 % 4) + w // 2)
    order = (mine * own_blocks + block) * 6 + face
    entry = jnp.full(shape, -1, jnp.int32)
    layer = place
    for k in range(6):
        layer = jnp.where(face == k, layer_voxel(k, place), layer)
        for b in range(own_blocks):
            entry = jnp.where(
                (block == b) & (face == k), nbr_ref[mine * own_blocks + b, k], entry
            )
    home = entry >> (block_count.bit_length() - 1)
    rank = jnp.zeros(shape, jnp.int32)
    for b in range(block_count):
        for k in range(6):
            other = nbr_ref[b, k] >> (block_count.bit_length() - 1)
            rank = rank + jnp.where((home == other) & (order > 6 * b + k), 1, 0)
    off = lax.rem(home - me + ranges, ranges)
    target = jnp.where(
        off == 0,
        (entry - me * block_count) * PIECE + layer,
        width + (off - 1) * FACE_CAP * LAYER + rank * LAYER + place,
    )
    target = jnp.where(entry >= 0, target, -1)
    return jnp.concatenate([target[g : g + 1] for g in range(shape[0])], axis=1)


def one_hot(depth, target, first=0):
    shape = (depth, target.shape[1])
    lanes = lax.broadcasted_iota(jnp.int32, shape, 0) + first
    return jnp.where(lanes == target, 1.0, 0.0).astype(jnp.bfloat16)


def each(count, body):
    if count <= 4:
        for i in range(count):
            body(i)
    else:
        lax.fori_loop(0, count, lambda i, c: (body(i), c)[1], 0)


def kernel(
    ranges,
    chans,
    dest_ref,
    nbr_ref,
    bias_ref,
    parents_hbm,
    up_hbm,
    conv_hbm,
    out_ref,
    parents_ref,
    up_ref,
    conv_ref,
    up_pairs,
    conv_wide,
    pick_inner,
    pick_outer,
    moves,
    moved,
    asks,
    asked,
    held,
    faces_out,
    faces_in,
    far_ref,
    cube,
    cols,
    load_sem,
    ask_send,
    ask_recv,
    move_send,
    move_recv,
    held_send,
    held_recv,
    face_send,
    face_recv,
):
    me = lax.axis_index("morton")
    mine = lax.axis_index("chan")
    total = ranges * chans
    own_blocks = out_ref.shape[0]
    block_count = nbr_ref.shape[0]
    parent_count, depth = parents_ref.shape[0], parents_ref.shape[1]
    half = depth // 2
    width = held.shape[2]
    move_width = MOVE_CAP * PIECE

    parents_load = pltpu.make_async_copy(parents_hbm, parents_ref, load_sem.at[2])
    up_load = pltpu.make_async_copy(up_hbm, up_ref, load_sem.at[0])
    conv_load = pltpu.make_async_copy(conv_hbm, conv_ref, load_sem.at[1])
    parents_load.start()
    up_load.start()
    conv_load.start()

    def at(range_id, chan_id):
        return {"morton": range_id, "chan": chan_id}

    barrier = pltpu.get_barrier_semaphore()
    here = me * chans + mine

    def greet(i):
        other = lax.rem(here + i + 1, total)
        pl.semaphore_signal(
            barrier, inc=1, device_id=at(other // chans, lax.rem(other, chans)), device_id_type=MESH
        )

    each(total - 1, greet)

    request = request_table(nbr_ref, ranges, me)
    for m in range(ranges - 1):
        asks[m] = request[m : m + 1]
    pick = pick_table(dest_ref, ranges, block_count, me)

    def gather(columns):
        found = jnp.zeros((depth, columns.shape[1]), jnp.float32)
        for p in range(parent_count):
            found = found + jnp.dot(
                parents_ref[p], one_hot(512, columns, 512 * p), preferred_element_type=jnp.float32
            )
        return found.astype(jnp.bfloat16)

    parents_load.wait()
    passed = gather(pick[:, width:])
    moves[0] = passed[:, :move_width]
    moves[1] = passed[:, move_width:]

    pl.semaphore_wait(barrier, total - 1)

    def ask_copy(m, arrives):
        return pltpu.make_async_remote_copy(
            src_ref=asks.at[m],
            dst_ref=asked.at[arrives],
            send_sem=ask_send.at[m],
            recv_sem=ask_recv.at[arrives],
            device_id=at(lax.rem(me + m + 1, ranges), mine),
            device_id_type=MESH,
        )

    def move_copy(side, i, source):
        other = lax.rem(me + (1 if side == 0 else ranges - 1), ranges)
        return pltpu.make_async_remote_copy(
            src_ref=moves.at[side],
            dst_ref=moved.at[side, source],
            send_sem=move_send.at[side, i],
            recv_sem=move_recv.at[side, i],
            device_id=at(other, lax.rem(mine + i, chans)),
            device_id_type=MESH,
        )

    def held_copy(i, source):
        return pltpu.make_async_remote_copy(
            src_ref=held.at[source],
            dst_ref=held.at[source],
            send_sem=held_send.at[i],
            recv_sem=held_recv.at[i],
            device_id=at(me, lax.rem(mine + i + 1, chans)),
            device_id_type=MESH,
        )

    each(ranges - 1, lambda m: ask_copy(m, ranges - 2 - m).start())

    gives = (me < ranges - 1, me > 0)
    takes = (me > 0, me < ranges - 1)
    for side in range(2):

        @pl.when(gives[side])
        def _():
            for i in range(chans):
                move_copy(side, i, mine).start()

        @pl.when(jnp.logical_not(takes[side]))
        def _():
            moved[side] = jnp.zeros(moved.shape[1:], jnp.bfloat16)

    gathered = gather(pick[:, :width])
    held[mine] = gathered
    each(chans - 1, lambda i: held_copy(i, mine).start())

    faces_in[ranges - 1] = jnp.zeros(faces_in.shape[1:], jnp.bfloat16)
    outer_rows = outer_table(nbr_ref, ranges, own_blocks, me, mine)
    pick_outer[...] = one_hot(pick_outer.shape[0], outer_rows)
    pick_inner[...] = one_hot(width, inner_table(block_count, own_blocks, mine))

    up_load.wait()
    for o in range(8):
        up_pairs[o // 2, :, 128 * (o % 2) : 128 * (o % 2 + 1)] = up_ref[o]
    conv_load.wait()
    for dx in range(3):
        conv_wide[:, 128 * dx : 128 * (dx + 1)] = conv_ref[9 * dx : 9 * dx + 9].reshape(1152, 128)

    def add_moved(block, low, high):
        first = block[:, :move_width].astype(jnp.float32) + low.astype(jnp.float32)
        last = block[:, width - move_width :].astype(jnp.float32) + high.astype(jnp.float32)
        return jnp.concatenate(
            [
                first.astype(jnp.bfloat16),
                block[:, move_width : width - move_width],
                last.astype(jnp.bfloat16),
            ],
            axis=1,
        )

    for side in range(2):

        @pl.when(takes[side])
        def _():
            move_copy(side, 0, mine).wait_recv()

    own = add_moved(gathered, moved[0, mine], moved[1, mine])

    def face_copy(m, i, arrives, source):
        return pltpu.make_async_remote_copy(
            src_ref=faces_out.at[m],
            dst_ref=faces_in.at[arrives, source],
            send_sem=face_send.at[m, i],
            recv_sem=face_recv.at[arrives, i],
            device_id=at(lax.rem(me + m + 1, ranges), lax.rem(mine + i, chans)),
            device_id_type=MESH,
        )

    def answer(first, count):
        ask = []
        for m in range(count):
            ask_copy(first + m, first + m).wait_recv()
            ask.append(asked[first + m][:, :PIECE])
        found = jnp.dot(
            own, one_hot(width, jnp.concatenate(ask, axis=1)), preferred_element_type=jnp.float32
        )
        for m in range(count):
            part = found[:, PIECE * m : PIECE * (m + 1)]
            faces_out[first + m] = jnp.concatenate([part[:half], part[half:]], axis=1).astype(
                jnp.bfloat16
            )
            for i in range(chans):
                face_copy(first + m, i, ranges - 2 - first - m, mine).start()

    if ranges <= 4:
        answer(0, ranges - 1)
    else:
        each(ranges - 1, lambda m: answer(m, 1))

    for i in range(1, chans):
        source = lax.rem(mine + chans - i, chans)
        for side in range(2):

            @pl.when(takes[side])
            def _():
                move_copy(side, i, source).wait_recv()

        held_copy(i - 1, source).wait_recv()
    near = add_moved(
        held[...].reshape(chans * depth, width),
        moved[0].reshape(chans * depth, move_width),
        moved[1].reshape(chans * depth, move_width),
    )

    count = own_blocks * 128
    z_at = lax.rem(lax.broadcasted_iota(jnp.int32, (128, 128), 0), 8)
    odd = lax.rem(lax.broadcasted_iota(jnp.int32, (count, 128), 0), 2) == 1
    outer_high = jnp.concatenate([odd, jnp.logical_not(odd)], axis=0)

    def lift(voxels, high):
        lifted = {}
        for ox in range(2):
            for oy in range(2):
                both = jnp.dot(voxels, up_pairs[2 * ox + oy], preferred_element_type=jnp.float32)
                lifted[ox, oy] = jnp.where(high, both[:, 128:], both[:, :128])
        return lifted

    inner = jnp.dot(near, pick_inner[...], preferred_element_type=jnp.float32)

    outer = jnp.dot(near, pick_outer[:width], preferred_element_type=jnp.float32)
    inner_up = lift(inner.T.astype(jnp.bfloat16), odd)

    def face_wait(m):
        for i in range(chans):
            face_copy(m, i, m, lax.rem(mine + chans - i, chans)).wait_recv()

    each(ranges - 1, face_wait)

    def unpack(m):
        both = faces_in[m].astype(jnp.float32)
        part = jnp.concatenate([both[:, :, :PIECE], both[:, :, PIECE:]], axis=1)
        return part.reshape(chans * depth, PIECE)

    def widen(i):
        first = i * 2 * PIECE if isinstance(i, int) else pl.multiple_of(i * 2 * PIECE, 2 * PIECE)
        far_ref[:, pl.ds(first, 2 * PIECE)] = jnp.concatenate(
            [unpack(2 * i), unpack(2 * i + 1)], axis=1
        ).astype(jnp.bfloat16)

    each(ranges // 2, widen)
    outer = outer + jnp.dot(
        far_ref[...],
        pick_outer[width:],
        preferred_element_type=jnp.float32,
    )
    outer_up = lift(outer.T.astype(jnp.bfloat16), outer_high)

    nothing = jnp.zeros((8, 128), jnp.float32)

    def shifts(middle, end):
        below = jnp.where(z_at == 0, end, pltpu.roll(middle, 1, 0))
        above = jnp.where(z_at == 7, end, pltpu.roll(middle, 127, 0))
        return below, middle, above

    for b in range(own_blocks):
        first = 128 * b
        for ox in range(2):
            for oy in range(2):
                outside = outer_up[ox, oy]
                inner = shifts(
                    inner_up[ox, oy][first : first + 128], outside[count + first : count + first + 128]
                )
                sides = shifts(outside[first : first + 128], 0.0)
                for dz in range(3):
                    for p in range(4):
                        for q in range(4):
                            at_row = 8 * (4 * p + q)
                            cube[dz, 1 + 2 * p + ox, 1 + 2 * q + oy] = inner[dz][at_row : at_row + 8]
                    for t in range(4):
                        face_x, face_y = 1 - ox, 3 - oy
                        low = 32 * face_x + 8 * t
                        cube[dz, 9 * face_x, 1 + 2 * t + oy] = sides[dz][low : low + 8]
                        low = 32 * face_y + 8 * t
                        cube[dz, 1 + 2 * t + ox, 9 * (face_y - 2)] = sides[dz][low : low + 8]
        for dz in range(3):
            for x in (0, 9):
                for y in (0, 9):
                    cube[dz, x, y] = nothing
        for x in range(10):
            for dy in range(3):
                for dz in range(3):
                    lane = 128 * (3 * dy + dz)
                    cols[x, :, lane : lane + 128] = (
                        cube[dz, x, dy : dy + 8].reshape(64, 128).astype(jnp.bfloat16)
                    )
        taps = jnp.dot(cols[...].reshape(640, 1152), conv_wide[...], preferred_element_type=jnp.float32)
        total_sum = taps[:512, :128] + taps[64:576, 128:256] + taps[128:, 256:] + bias_ref[...]
        result = total_sum / (1.0 + jnp.exp(-total_sum))
        out_ref[b] = result.T.astype(jnp.bfloat16)

    def finish(m):
        ask_copy(m, m).wait_send()
        for i in range(chans):
            face_copy(m, i, m, mine).wait_send()

    each(ranges - 1, finish)
    for i in range(chans):
        for side in range(2):

            @pl.when(gives[side])
            def _():
                move_copy(side, i, mine).wait_send()

        if i > 0:
            held_copy(i - 1, mine).wait_send()


def per_device(parents, up_weight, conv_weight, conv_bias, child_dest, face_nbr):
    ranges, chans = lax.axis_size("morton"), lax.axis_size("chan")
    block_count = face_nbr.shape[0]
    own_blocks = block_count // chans
    depth = parents.shape[1]
    width = block_count * PIECE
    vmem = pl.BlockSpec(memory_space=pltpu.VMEM)
    smem = pl.BlockSpec(memory_space=pltpu.SMEM)
    hbm = pl.BlockSpec(memory_space=pltpu.HBM)
    ask_shape = (ranges - 1, 1, 2 * FACE_CAP * LAYER)
    far_width = ranges * FACE_CAP * LAYER
    bf16 = jnp.bfloat16
    dma = pltpu.SemaphoreType.DMA
    return pl.pallas_call(
        functools.partial(kernel, ranges, chans),
        out_shape=pltpu.VMEM((own_blocks, 128, 512), bf16),
        in_specs=[smem] * 2 + [vmem] + [hbm] * 3,
        out_specs=vmem,
        scratch_shapes=[
            pltpu.VMEM(parents.shape, bf16),
            pltpu.VMEM(up_weight.shape, bf16),
            pltpu.VMEM(conv_weight.shape, bf16),
            pltpu.VMEM((4, 256, 256), bf16),
            pltpu.VMEM((1152, 384), bf16),
            pltpu.VMEM((width, own_blocks * 128), bf16),
            pltpu.VMEM((width + far_width, own_blocks * 256), bf16),
            pltpu.VMEM((2, depth, MOVE_CAP * PIECE), bf16),
            pltpu.VMEM((2, chans, depth, MOVE_CAP * PIECE), bf16),
            pltpu.VMEM(ask_shape, jnp.int32),
            pltpu.VMEM(ask_shape, jnp.int32),
            pltpu.VMEM((chans, depth, width), bf16),
            pltpu.VMEM((ranges - 1, depth // 2, 2 * PIECE), bf16),
            pltpu.VMEM((ranges, chans, depth // 2, 2 * PIECE), bf16),
            pltpu.VMEM((chans * depth, ranges * PIECE), bf16),
            pltpu.VMEM((3, 10, 10, 8, 128), jnp.float32),
            pltpu.VMEM((10, 64, 1152), bf16),
            dma((3,)),
            dma((ranges - 1,)),
            dma((ranges - 1,)),
            dma((2, chans)),
            dma((2, chans)),
            dma((chans - 1,)),
            dma((chans - 1,)),
            dma((ranges - 1, chans)),
            dma((ranges - 1, chans)),
        ],
        compiler_params=pltpu.CompilerParams(
            collective_id=0, has_side_effects=True, vmem_limit_bytes=56 * 1024 * 1024
        ),
        name="sparse_level",
    )(child_dest, face_nbr, conv_bias.reshape(1, -1), parents, up_weight, conv_weight)


def solution(mesh):
    placed = (
        P(("groups", "morton"), "chan", None),
        P(),
        P(),
        P(),
        P(("groups", "morton")),
        P(("groups", "morton"), None),
    )
    return jax.shard_map(
        per_device,
        mesh=mesh,
        in_specs=placed,
        out_specs=P(("groups", "morton", "chan"), None, None),
        check_vma=False,
    )
```

```python
import functools

import jax
import jax.numpy as jnp
from jax import lax
from jax.experimental import pallas as pl
from jax.experimental.pallas import tpu as pltpu
from jax.sharding import PartitionSpec as P

MOVE_CAP = 2
FACE_CAP = 4
PIECE = 64
LAYER = 16
MESH = pl.DeviceIdType.MESH


def lane_ids(width, rows=1):
    return lax.broadcasted_iota(jnp.int32, (rows, width), 1)


def layer_voxel(face, place):
    p, q = place >> 2, place & 3
    return (
        lambda: 48 + place,
        lambda: place,
        lambda: 16 * p + 12 + q,
        lambda: 16 * p + q,
        lambda: 4 * place + 3,
        lambda: 4 * place,
    )[face]()


def pick_table(dest_ref, ranges, block_count, me):
    slots = block_count + 2 * MOVE_CAP
    lane = lane_ids(slots * PIECE)
    slot, v = lane // PIECE, lane % PIECE
    slot = jnp.where(slot < block_count + MOVE_CAP, slot, slot - slots)
    wanted = me * block_count + slot
    wanted = jnp.where(wanted < 0, -9, wanted)
    base = 64 * (v // 16) + 8 * (v // 4 % 4) + v % 4
    pick = jnp.full(lane.shape, -1, jnp.int32)
    for c in range(dest_ref.shape[0]):
        k = c % 8
        first = 512 * (c // 8) + 256 * (k % 2) + 32 * (k // 2 % 2) + 4 * (k // 4)
        pick = jnp.where(wanted == dest_ref[c], base + first, pick)
    return pick


def request_table(nbr_ref, ranges, me):
    block_count = nbr_ref.shape[0]
    shape = (ranges - 1, 2 * FACE_CAP * LAYER)
    lane = lane_ids(shape[1], shape[0])
    slot, place = lane // LAYER, lane % LAYER
    home = lax.rem(me + 1 + lax.broadcasted_iota(jnp.int32, shape, 0), ranges)
    layers = [layer_voxel(k, place) for k in range(6)]
    seen = jnp.zeros(shape, jnp.int32)
    ask = jnp.full(shape, -1, jnp.int32)
    for b in range(block_count):
        for k in range(6):
            start = nbr_ref[b, k] - home * block_count
            hit = (start >= 0) & (start < block_count)
            ask = jnp.where(hit & (seen == slot), start * PIECE + layers[k], ask)
            seen = seen + jnp.where(hit, 1, 0)
    return ask


def inner_table(block_count, own_blocks, mine):
    lane = lane_ids(128)
    return jnp.concatenate(
        [PIECE * (mine * own_blocks + b) + 4 * (lane // 8) + lane % 8 // 2 for b in range(own_blocks)],
        axis=1,
    )


def outer_table(nbr_ref, ranges, own_blocks, me, mine):
    block_count = nbr_ref.shape[0]
    width = block_count * PIECE
    shape = (2 * own_blocks, 128)
    lane = lane_ids(128, shape[0])
    group = lax.broadcasted_iota(jnp.int32, shape, 0)
    w = lane % 8
    end = group >= own_blocks
    block = jnp.where(end, group - own_blocks, group)
    face = jnp.where(end, jnp.where(w == 0, 4, jnp.where(w == 7, 5, 6)), lane // 32)
    place = jnp.where(end, lane // 8, 4 * (lane // 8 % 4) + w // 2)
    order = (mine * own_blocks + block) * 6 + face
    entry = jnp.full(shape, -1, jnp.int32)
    layer = place
    for k in range(6):
        layer = jnp.where(face == k, layer_voxel(k, place), layer)
        for b in range(own_blocks):
            entry = jnp.where(
                (block == b) & (face == k), nbr_ref[mine * own_blocks + b, k], entry
            )
    home = entry >> (block_count.bit_length() - 1)
    rank = jnp.zeros(shape, jnp.int32)
    for b in range(block_count):
        for k in range(6):
            other = nbr_ref[b, k] >> (block_count.bit_length() - 1)
            rank = rank + jnp.where((home == other) & (order > 6 * b + k), 1, 0)
    off = lax.rem(home - me + ranges, ranges)
    target = jnp.where(
        off == 0,
        (entry - me * block_count) * PIECE + layer,
        width + (off - 1) * FACE_CAP * LAYER + rank * LAYER + place,
    )
    target = jnp.where(entry >= 0, target, -1)
    return jnp.concatenate([target[g : g + 1] for g in range(shape[0])], axis=1)


def one_hot(depth, target, first=0):
    shape = (depth, target.shape[1])
    lanes = lax.broadcasted_iota(jnp.int32, shape, 0) + first
    return jnp.where(lanes == target, 1.0, 0.0).astype(jnp.bfloat16)


def each(count, body):
    if count <= 4:
        for i in range(count):
            body(i)
    else:
        lax.fori_loop(0, count, lambda i, c: (body(i), c)[1], 0)


def kernel(
    ranges,
    chans,
    dest_ref,
    nbr_ref,
    bias_ref,
    parents_hbm,
    up_hbm,
    conv_hbm,
    out_ref,
    parents_ref,
    up_ref,
    conv_ref,
    up_pairs,
    conv_wide,
    pick_inner,
    pick_outer,
    moves,
    moved,
    asks,
    asked,
    held,
    faces_out,
    faces_in,
    far_ref,
    cube,
    cols,
    load_sem,
    ask_send,
    ask_recv,
    move_send,
    move_recv,
    held_send,
    held_recv,
    face_send,
    face_recv,
):
    me = lax.axis_index("morton")
    mine = lax.axis_index("chan")
    total = ranges * chans
    own_blocks = out_ref.shape[0]
    block_count = nbr_ref.shape[0]
    parent_count, depth = parents_ref.shape[0], parents_ref.shape[1]
    half = depth // 2
    width = held.shape[2]
    move_width = MOVE_CAP * PIECE

    parents_load = pltpu.make_async_copy(parents_hbm, parents_ref, load_sem.at[2])
    up_load = pltpu.make_async_copy(up_hbm, up_ref, load_sem.at[0])
    conv_load = pltpu.make_async_copy(conv_hbm, conv_ref, load_sem.at[1])
    parents_load.start()
    up_load.start()
    conv_load.start()

    def at(range_id, chan_id):
        return {"morton": range_id, "chan": chan_id}

    barrier = pltpu.get_barrier_semaphore()
    here = me * chans + mine

    def greet(i):
        other = lax.rem(here + i + 1, total)
        pl.semaphore_signal(
            barrier, inc=1, device_id=at(other // chans, lax.rem(other, chans)), device_id_type=MESH
        )

    each(total - 1, greet)

    request = request_table(nbr_ref, ranges, me)
    for m in range(ranges - 1):
        asks[m] = request[m : m + 1]
    pick = pick_table(dest_ref, ranges, block_count, me)

    def gather(columns):
        found = jnp.zeros((depth, columns.shape[1]), jnp.float32)
        for p in range(parent_count):
            found = found + jnp.dot(
                parents_ref[p], one_hot(512, columns, 512 * p), preferred_element_type=jnp.float32
            )
        return found.astype(jnp.bfloat16)

    parents_load.wait()
    passed = gather(pick[:, width:])
    moves[0] = passed[:, :move_width]
    moves[1] = passed[:, move_width:]

    pl.semaphore_wait(barrier, total - 1)

    def ask_copy(m, arrives):
        return pltpu.make_async_remote_copy(
            src_ref=asks.at[m],
            dst_ref=asked.at[arrives],
            send_sem=ask_send.at[m],
            recv_sem=ask_recv.at[arrives],
            device_id=at(lax.rem(me + m + 1, ranges), mine),
            device_id_type=MESH,
        )

    def move_copy(side, i, source):
        other = lax.rem(me + (1 if side == 0 else ranges - 1), ranges)
        return pltpu.make_async_remote_copy(
            src_ref=moves.at[side],
            dst_ref=moved.at[side, source],
            send_sem=move_send.at[side, i],
            recv_sem=move_recv.at[side, i],
            device_id=at(other, lax.rem(mine + i, chans)),
            device_id_type=MESH,
        )

    def held_copy(i, source):
        return pltpu.make_async_remote_copy(
            src_ref=held.at[source],
            dst_ref=held.at[source],
            send_sem=held_send.at[i],
            recv_sem=held_recv.at[i],
            device_id=at(me, lax.rem(mine + i + 1, chans)),
            device_id_type=MESH,
        )

    each(ranges - 1, lambda m: ask_copy(m, ranges - 2 - m).start())

    gives = (me < ranges - 1, me > 0)
    takes = (me > 0, me < ranges - 1)
    for side in range(2):

        @pl.when(gives[side])
        def _():
            for i in range(chans):
                move_copy(side, i, mine).start()

        @pl.when(jnp.logical_not(takes[side]))
        def _():
            moved[side] = jnp.zeros(moved.shape[1:], jnp.bfloat16)

    gathered = gather(pick[:, :width])
    held[mine] = gathered
    each(chans - 1, lambda i: held_copy(i, mine).start())

    faces_in[ranges - 1] = jnp.zeros(faces_in.shape[1:], jnp.bfloat16)
    outer_rows = outer_table(nbr_ref, ranges, own_blocks, me, mine)
    pick_outer[...] = one_hot(pick_outer.shape[0], outer_rows)
    pick_inner[...] = one_hot(width, inner_table(block_count, own_blocks, mine))

    up_load.wait()
    for o in range(8):
        up_pairs[o // 2, :, 128 * (o % 2) : 128 * (o % 2 + 1)] = up_ref[o]
    conv_load.wait()
    for dx in range(3):
        conv_wide[:, 128 * dx : 128 * (dx + 1)] = conv_ref[9 * dx : 9 * dx + 9].reshape(1152, 128)

    def add_moved(block, low, high):
        first = block[:, :move_width].astype(jnp.float32) + low.astype(jnp.float32)
        last = block[:, width - move_width :].astype(jnp.float32) + high.astype(jnp.float32)
        return jnp.concatenate(
            [
                first.astype(jnp.bfloat16),
                block[:, move_width : width - move_width],
                last.astype(jnp.bfloat16),
            ],
            axis=1,
        )

    for side in range(2):

        @pl.when(takes[side])
        def _():
            move_copy(side, 0, mine).wait_recv()

    own = add_moved(gathered, moved[0, mine], moved[1, mine])

    def face_copy(m, i, arrives, source):
        return pltpu.make_async_remote_copy(
            src_ref=faces_out.at[m],
            dst_ref=faces_in.at[arrives, source],
            send_sem=face_send.at[m, i],
            recv_sem=face_recv.at[arrives, i],
            device_id=at(lax.rem(me + m + 1, ranges), lax.rem(mine + i, chans)),
            device_id_type=MESH,
        )

    def answer(first, count):
        ask = []
        for m in range(count):
            ask_copy(first + m, first + m).wait_recv()
            ask.append(asked[first + m][:, :PIECE])
        found = jnp.dot(
            own, one_hot(width, jnp.concatenate(ask, axis=1)), preferred_element_type=jnp.float32
        )
        for m in range(count):
            part = found[:, PIECE * m : PIECE * (m + 1)]
            faces_out[first + m] = jnp.concatenate([part[:half], part[half:]], axis=1).astype(
                jnp.bfloat16
            )
            for i in range(chans):
                face_copy(first + m, i, ranges - 2 - first - m, mine).start()

    if ranges <= 4:
        answer(0, ranges - 1)
    else:
        each(ranges - 1, lambda m: answer(m, 1))

    for i in range(1, chans):
        source = lax.rem(mine + chans - i, chans)
        for side in range(2):

            @pl.when(takes[side])
            def _():
                move_copy(side, i, source).wait_recv()

        held_copy(i - 1, source).wait_recv()
    near = add_moved(
        held[...].reshape(chans * depth, width),
        moved[0].reshape(chans * depth, move_width),
        moved[1].reshape(chans * depth, move_width),
    )

    count = own_blocks * 128
    z_at = lax.rem(lax.broadcasted_iota(jnp.int32, (128, 128), 0), 8)
    odd = lax.rem(lax.broadcasted_iota(jnp.int32, (count, 128), 0), 2) == 1
    outer_high = jnp.concatenate([odd, jnp.logical_not(odd)], axis=0)

    def lift(voxels, high):
        lifted = {}
        for ox in range(2):
            for oy in range(2):
                both = jnp.dot(voxels, up_pairs[2 * ox + oy], preferred_element_type=jnp.float32)
                lifted[ox, oy] = jnp.where(high, both[:, 128:], both[:, :128])
        return lifted

    inner = jnp.dot(near, pick_inner[...], preferred_element_type=jnp.float32)

    outer = jnp.dot(near, pick_outer[:width], preferred_element_type=jnp.float32)
    inner_up = lift(inner.T.astype(jnp.bfloat16), odd)

    nothing = jnp.zeros((8, 128), jnp.float32)
    for b in range(own_blocks):
        for dz in range(3):
            for x in (0, 9):
                for y in (0, 9):
                    cube[b, dz, x, y] = nothing
        for ox in range(2):
            for oy in range(2):
                for p in range(4):
                    for q in range(4):
                        at_row = 128 * b + 8 * (4 * p + q)
                        cube[b, 1, 1 + 2 * p + ox, 1 + 2 * q + oy] = inner_up[ox, oy][at_row : at_row + 8]

    def face_wait(m):
        for i in range(chans):
            face_copy(m, i, m, lax.rem(mine + chans - i, chans)).wait_recv()

    each(ranges - 1, face_wait)

    def unpack(m):
        both = faces_in[m].astype(jnp.float32)
        part = jnp.concatenate([both[:, :, :PIECE], both[:, :, PIECE:]], axis=1)
        return part.reshape(chans * depth, PIECE)

    def widen(i):
        first = i * 2 * PIECE if isinstance(i, int) else pl.multiple_of(i * 2 * PIECE, 2 * PIECE)
        far_ref[:, pl.ds(first, 2 * PIECE)] = jnp.concatenate(
            [unpack(2 * i), unpack(2 * i + 1)], axis=1
        ).astype(jnp.bfloat16)

    each(ranges // 2, widen)
    outer = outer + jnp.dot(
        far_ref[...],
        pick_outer[width:],
        preferred_element_type=jnp.float32,
    )
    outer_up = lift(outer.T.astype(jnp.bfloat16), outer_high)

    def shifts(middle, end):
        below = jnp.where(z_at == 0, end, pltpu.roll(middle, 1, 0))
        above = jnp.where(z_at == 7, end, pltpu.roll(middle, 127, 0))
        return below, middle, above

    for b in range(own_blocks):
        first = 128 * b
        for ox in range(2):
            for oy in range(2):
                outside = outer_up[ox, oy]
                inner = shifts(
                    inner_up[ox, oy][first : first + 128], outside[count + first : count + first + 128]
                )
                sides = shifts(outside[first : first + 128], 0.0)
                for dz in range(3):
                    for p in range(4 if dz != 1 else 0):
                        for q in range(4):
                            at_row = 8 * (4 * p + q)
                            cube[b, dz, 1 + 2 * p + ox, 1 + 2 * q + oy] = inner[dz][at_row : at_row + 8]
                    for t in range(4):
                        face_x, face_y = 1 - ox, 3 - oy
                        low = 32 * face_x + 8 * t
                        cube[b, dz, 9 * face_x, 1 + 2 * t + oy] = sides[dz][low : low + 8]
                        low = 32 * face_y + 8 * t
                        cube[b, dz, 1 + 2 * t + ox, 9 * (face_y - 2)] = sides[dz][low : low + 8]
        for x in range(10):
            for dy in range(3):
                for dz in range(3):
                    lane = 128 * (3 * dy + dz)
                    cols[b, x, :, lane : lane + 128] = (
                        cube[b, dz, x, dy : dy + 8].reshape(64, 128).astype(jnp.bfloat16)
                    )
    taps = jnp.dot(
        cols[...].reshape(own_blocks * 640, 1152), conv_wide[...], preferred_element_type=jnp.float32
    )
    for b in range(own_blocks):
        rows = taps[640 * b : 640 * (b + 1)]
        total_sum = rows[:512, :128] + rows[64:576, 128:256] + rows[128:, 256:] + bias_ref[...]
        result = total_sum / (1.0 + jnp.exp(-total_sum))
        out_ref[b] = result.T.astype(jnp.bfloat16)

    def finish(m):
        ask_copy(m, m).wait_send()
        for i in range(chans):
            face_copy(m, i, m, mine).wait_send()

    each(ranges - 1, finish)
    for i in range(chans):
        for side in range(2):

            @pl.when(gives[side])
            def _():
                move_copy(side, i, mine).wait_send()

        if i > 0:
            held_copy(i - 1, mine).wait_send()


def per_device(parents, up_weight, conv_weight, conv_bias, child_dest, face_nbr):
    ranges, chans = lax.axis_size("morton"), lax.axis_size("chan")
    block_count = face_nbr.shape[0]
    own_blocks = block_count // chans
    depth = parents.shape[1]
    width = block_count * PIECE
    vmem = pl.BlockSpec(memory_space=pltpu.VMEM)
    smem = pl.BlockSpec(memory_space=pltpu.SMEM)
    hbm = pl.BlockSpec(memory_space=pltpu.HBM)
    ask_shape = (ranges - 1, 1, 2 * FACE_CAP * LAYER)
    far_width = ranges * FACE_CAP * LAYER
    bf16 = jnp.bfloat16
    dma = pltpu.SemaphoreType.DMA
    return pl.pallas_call(
        functools.partial(kernel, ranges, chans),
        out_shape=pltpu.VMEM((own_blocks, 128, 512), bf16),
        in_specs=[smem] * 2 + [vmem] + [hbm] * 3,
        out_specs=vmem,
        scratch_shapes=[
            pltpu.VMEM(parents.shape, bf16),
            pltpu.VMEM(up_weight.shape, bf16),
            pltpu.VMEM(conv_weight.shape, bf16),
            pltpu.VMEM((4, 256, 256), bf16),
            pltpu.VMEM((1152, 384), bf16),
            pltpu.VMEM((width, own_blocks * 128), bf16),
            pltpu.VMEM((width + far_width, own_blocks * 256), bf16),
            pltpu.VMEM((2, depth, MOVE_CAP * PIECE), bf16),
            pltpu.VMEM((2, chans, depth, MOVE_CAP * PIECE), bf16),
            pltpu.VMEM(ask_shape, jnp.int32),
            pltpu.VMEM(ask_shape, jnp.int32),
            pltpu.VMEM((chans, depth, width), bf16),
            pltpu.VMEM((ranges - 1, depth // 2, 2 * PIECE), bf16),
            pltpu.VMEM((ranges, chans, depth // 2, 2 * PIECE), bf16),
            pltpu.VMEM((chans * depth, ranges * PIECE), bf16),
            pltpu.VMEM((own_blocks, 3, 10, 10, 8, 128), jnp.float32),
            pltpu.VMEM((own_blocks, 10, 64, 1152), bf16),
            dma((3,)),
            dma((ranges - 1,)),
            dma((ranges - 1,)),
            dma((2, chans)),
            dma((2, chans)),
            dma((chans - 1,)),
            dma((chans - 1,)),
            dma((ranges - 1, chans)),
            dma((ranges - 1, chans)),
        ],
        compiler_params=pltpu.CompilerParams(
            collective_id=0, has_side_effects=True, vmem_limit_bytes=56 * 1024 * 1024
        ),
        name="sparse_level",
    )(child_dest, face_nbr, conv_bias.reshape(1, -1), parents, up_weight, conv_weight)


def solution(mesh):
    placed = (
        P(("groups", "morton"), "chan", None),
        P(),
        P(),
        P(),
        P(("groups", "morton")),
        P(("groups", "morton"), None),
    )
    return jax.shard_map(
        per_device,
        mesh=mesh,
        in_specs=placed,
        out_specs=P(("groups", "morton", "chan"), None, None),
        check_vma=False,
    )
```
